1024 devices in a mesh: fourier: 64 (over y, x, core), elem: 16 (over z).
Axes of the slice: x: 4, y: 8, z: 16, core: 2. Of those that a mesh axis runs over, the one named last changes fastest.
Arguments:
- vel_az: float32 [256, 2048, 256], P('fourier', 'elem'), may hold values from -1.5 to 1.5
- vel_rad: float32 [256, 2048, 256], P('fourier', 'elem'), may hold values from -1.5 to 1.5
- axial: float32 [256, 2048, 256], P('fourier', 'elem'), may hold values from -6 to 6
- metric_az: float32 [256, 32], P('elem'), may hold values from 0.4 to 2.5
- metric_rad: float32 [256, 32], P('elem'), may hold values from 0.4 to 2.5
Outputs:
- velocity_modes: float32 [256, 2048, 256], P('fourier', 'elem')
The draws below stay inside these ranges and needn't reach their ends.
All inputs are finite; a program needn't handle non-finite values.
Results may differ from the reference program's by a relative error of at most 0.0001.
Values sent between devices are 32-bit elements; how exact they have to be, the bound alone decides.
A program may use at most 32 MiB of HBM per device.

```python
import math
import jax
import jax.numpy as jnp
import numpy as np
from jax import lax

PLANES = 256
NODES = 8
ER = 32
ITERS = 2
EA = 256
NA = 2048
NR = 256


def level_of(rng, shape, pieces, smallest, high):
    level = 1.0
    for dim, parts in pieces:
        heights = jax.random.uniform(jax.random.fold_in(jax.random.fold_in(rng, 6), dim), (parts,), jnp.float32, smallest / len(pieces), high / len(pieces))
        level = level * jnp.repeat(jnp.exp(heights), shape[dim] // parts).reshape((-1,) + (1,) * (len(shape) - 1 - dim))
    return level


def gaussian(key, extent, deviation, bound, cuts=(), held_as=jnp.bfloat16):
    result = deviation * jax.random.normal(key, extent, jnp.float32)
    if cuts:
        result = result * level_of(key, extent, cuts, -0.22, 0.18)
    return jnp.clip(result, -bound, bound).astype(held_as)


def setup_inputs(seed: int = 0) -> dict:
    splits = jax.random.split(jax.random.key(seed), 6)
    return {
        "vel_az": gaussian(splits[0], (PLANES, NA, NR), 0.25, 1.5, ((0, 64), (1, 16)), jnp.float32),
        "vel_rad": gaussian(splits[1], (PLANES, NA, NR), 0.25, 1.5, ((0, 64), (1, 16)), jnp.float32),
        "axial": gaussian(splits[2], (PLANES, NA, NR), 1.0, 6.0, ((0, 64), (1, 16)), jnp.float32),
        "metric_az": jnp.clip(jnp.exp(math.log(2.5) - 1.8325814 * jax.random.uniform(splits[3], (EA, ER), jnp.float32) ** level_of(splits[3], (EA, ER), ((0, 16),), -0.2, 0.2)), 0.4, 2.5),
        "metric_rad": jnp.clip(jnp.exp(math.log(2.5) - 1.8325814 * jax.random.uniform(splits[4], (EA, ER), jnp.float32) ** level_of(splits[4], (EA, ER), ((0, 16),), -0.2, 0.2)), 0.4, 2.5),
    }


INV_DT = 2.0
INV_NU = 2.0
SHIFT = 4.0
BETA_UNIT = 0.03125
HIGH = lax.Precision.HIGHEST

def gll_tables():
    points = np.array([-1.0, -0.8717401485096066, -0.5917001814331423, -0.2092992179024789, 0.2092992179024789, 0.5917001814331423, 0.8717401485096066, 1.0])
    gll_weights = np.array([0.03571428571428571, 0.2107042271435061, 0.3411226924835044, 0.4124587946587038, 0.4124587946587038, 0.3411226924835044, 0.2107042271435061, 0.03571428571428571])
    number = points.shape[0]
    scales = np.array([np.prod([points[col_at] - points[other] for other in range(number) if other != col_at]) for col_at in range(number)])
    derivative = np.zeros((number, number))
    for row_at in range(number):
        for col_at in range(number):
            if row_at != col_at:
                derivative[row_at, col_at] = scales[row_at] / (scales[col_at] * (points[row_at] - points[col_at]))
    for row_at in range(number):
        derivative[row_at, row_at] = -np.sum(derivative[row_at])
    stiffness = derivative.T @ (gll_weights[:, None] * derivative)
    return (jnp.asarray(gll_weights, jnp.float32), jnp.asarray(derivative, jnp.float32), jnp.asarray(stiffness, jnp.float32))

def mode_table(planes):
    mode_ids = jnp.arange(planes, dtype=jnp.int32)
    waves = jnp.where(mode_ids == 1, planes // 2, mode_ids // 2)
    plane_ids = jnp.arange(planes, dtype=jnp.int32)
    phase = waves[:, None] * plane_ids[None, :] % planes
    angles = phase.astype(jnp.float32) * (2.0 * math.pi / planes)
    odd_rows = (mode_ids % 2 == 1) & (mode_ids > 1)
    table = jnp.where(odd_rows[:, None], -jnp.sin(angles), jnp.cos(angles))
    return table / math.sqrt(planes)

def reference(vel_az, vel_rad, axial, metric_az, metric_rad):
    gll_weights, derivative, stiffness = gll_tables()
    planes = axial.shape[0]
    elem_az, elem_rad = metric_az.shape
    five_dims = (planes, elem_az, NODES, elem_rad, NODES)
    metric_a = metric_az[None, :, None, :, None]
    metric_r = metric_rad[None, :, None, :, None]
    axial_cells = axial.reshape(five_dims)
    grad_az = jnp.einsum('ab,pibjr->piajr', derivative, axial_cells, precision=HIGH) * metric_a
    grad_rad = jnp.einsum('rs,piajs->piajr', derivative, axial_cells, precision=HIGH) * metric_r
    nonlinear = vel_az.reshape(five_dims) * grad_az + vel_rad.reshape(five_dims) * grad_rad
    drive = (INV_DT * axial_cells - nonlinear) * INV_NU
    table = mode_table(planes)
    spectral = jnp.dot(table, drive.reshape(planes, -1), precision=HIGH).reshape(five_dims)
    weight_a = gll_weights[None, None, :, None, None]
    weight_r = gll_weights[None, None, None, None, :]
    area = 1.0 / (metric_a * metric_r)
    mass_nodes = weight_a * weight_r * area
    coef_az = metric_a / metric_r * weight_r
    coef_rad = metric_r / metric_a * weight_a
    node_ids = jnp.arange(NODES, dtype=jnp.int32)
    elem_ids = jnp.arange(elem_rad, dtype=jnp.int32)
    wall = (elem_ids[:, None] == elem_rad - 1) & (node_ids[None, :] == NODES - 1)
    keep = jnp.where(wall, 0.0, 1.0).astype(jnp.float32)[None, None, None]
    edge_a = (node_ids == 0) | (node_ids == NODES - 1)
    count_a = jnp.where(edge_a, 2.0, 1.0).astype(jnp.float32)[None, None, :, None, None]
    shared_r = (node_ids[None, :] == NODES - 1) & (elem_ids[:, None] < elem_rad - 1) | (node_ids[None, :] == 0) & (elem_ids[:, None] > 0)
    count_r = jnp.where(shared_r, 2.0, 1.0).astype(jnp.float32)[None, None, None]
    inner_weight = 1.0 / (count_a * count_r)
    mode_ids = jnp.arange(planes, dtype=jnp.int32)
    waves = jnp.where(mode_ids == 1, planes // 2, mode_ids // 2)
    shift_coef = (SHIFT + (waves.astype(jnp.float32) * BETA_UNIT) ** 2)[:, None, None, None, None]

    def assemble(field):
        paired = field[..., :-1, NODES - 1] + field[..., 1:, 0]
        field = field.at[..., :-1, NODES - 1].set(paired).at[..., 1:, 0].set(paired)
        seam = field[:, :, NODES - 1] + jnp.roll(field[:, :, 0], -1, axis=1)
        field = field.at[:, :, NODES - 1].set(seam).at[:, :, 0].set(jnp.roll(seam, 1, axis=1))
        return field

    def operate(field):
        along_az = jnp.einsum('ab,mibjr->miajr', stiffness, field, precision=HIGH) * coef_az
        along_rad = jnp.einsum('rs,miajs->miajr', stiffness, field, precision=HIGH) * coef_rad
        return assemble(along_az + along_rad + shift_coef * mass_nodes * field) * keep

    def inner(left, right):
        return lax.optimization_barrier(jnp.sum(inner_weight * left * right, axis=(1, 2, 3, 4)))

    def widen(values):
        return values[:, None, None, None, None]
    right_side = assemble(mass_nodes * spectral) * keep
    solution = jnp.zeros_like(right_side)
    residual = right_side
    direction = right_side
    norm_now = inner(residual, residual)
    for iteration in range(ITERS):
        image = operate(direction)
        alpha = norm_now / inner(direction, image)
        solution = solution + widen(alpha) * direction
        residual = residual - widen(alpha) * image
        norm_next = inner(residual, residual)
        direction = residual + widen(norm_next / norm_now) * direction
        norm_now = norm_next
    return solution.reshape(planes, elem_az * NODES, elem_rad * NODES)
```

```python
import math

import jax
import jax.numpy as jnp
import ml_dtypes
import numpy as np
from jax import lax
from jax.experimental import pallas as pl
from jax.experimental.pallas import tpu as pltpu
from jax.sharding import PartitionSpec as P

MESH = pl.DeviceIdType.MESH
F32 = jnp.float32
BF16 = jnp.bfloat16
HIGH = lax.Precision.HIGHEST

PLANES = 256
NODES = 8
NF = 64
NZ = 16
ROWS = 128
COLS = 256
EZ = 16
UNIQUE = 7 * EZ
A_UNITS = 56
X_UNIT = 56
B_BASE = 57
UNITS = 99
PADDED = 105
FIRST = 64
EXTRA = (1, 27, 45)
SEAM = (0, 56, 57, 58, 59)

DR_H, DR_L, KR_H, KR_L, SR, ER, C_H, C_L = range(8)
DA_H, DA_L, KA_H, KA_L, RA_A, RA_B, EA_A, EA_B = range(8)


def gll_tables():
    points = np.array(
        [
            -1.0,
            -0.8717401485096066,
            -0.5917001814331423,
            -0.2092992179024789,
            0.2092992179024789,
            0.5917001814331423,
            0.8717401485096066,
            1.0,
        ]
    )
    gll_weights = np.array(
        [
            0.03571428571428571,
            0.2107042271435061,
            0.3411226924835044,
            0.4124587946587038,
            0.4124587946587038,
            0.3411226924835044,
            0.2107042271435061,
            0.03571428571428571,
        ]
    )
    number = points.shape[0]
    scales = np.array(
        [
            np.prod([points[col_at] - points[other] for other in range(number) if other != col_at])
            for col_at in range(number)
        ]
    )
    derivative = np.zeros((number, number))
    for row_at in range(number):
        for col_at in range(number):
            if row_at != col_at:
                derivative[row_at, col_at] = scales[row_at] / (
                    scales[col_at] * (points[row_at] - points[col_at])
                )
    for row_at in range(number):
        derivative[row_at, row_at] = -np.sum(derivative[row_at])
    stiffness = derivative.T @ (gll_weights[:, None] * derivative)
    return (
        gll_weights.astype(np.float32),
        derivative.astype(np.float32),
        stiffness.astype(np.float32),
    )


def mode_table():
    modes = np.arange(PLANES)
    waves = np.where(modes == 1, PLANES // 2, modes // 2)
    phase = waves[:, None] * np.arange(PLANES)[None, :] % PLANES
    angles = phase * (2.0 * math.pi / PLANES)
    odd = (modes % 2 == 1) & (modes > 1)
    return (np.where(odd[:, None], -np.sin(angles), np.cos(angles)) / math.sqrt(PLANES)).astype(
        np.float32
    )


def halves(matrix):
    high = matrix.astype(ml_dtypes.bfloat16)
    low = (matrix - high.astype(np.float32)).astype(ml_dtypes.bfloat16)
    return [high, low]


def row_maps():
    every = [(e, j) for e in range(EZ) for j in range(7)]
    first = {}
    for j in range(7):
        first[j] = (0, j)
        first[A_UNITS + j] = (EZ - 1, j)
    first[7] = (1, 0)
    left = [r for r in every if r not in first.values()]
    for at in range(2 * A_UNITS):
        if at not in first:
            first[at] = left.pop(0)
    second = {}
    for g in range(2):
        for q in range(4):
            j = g * 4 + q
            second[q * 16 + g] = (0, j) if j < 7 else (1, 0)
            if j < 7:
                second[(4 + q) * 16 + g] = (EZ - 1, j)
    left = [r for r in every if r not in second.values()]
    for block in range(8):
        for g in range(14):
            if block * 16 + g not in second:
                second[block * 16 + g] = left.pop(0)
    return first, second


def tables():
    weights, derivative, stiffness = gll_tables()
    w256, w128 = [], []
    w256 += halves(np.kron(np.eye(32, dtype=np.float32), derivative).T)
    w256 += halves(np.kron(np.eye(32, dtype=np.float32), stiffness).T)
    fold = np.zeros((COLS, COLS), np.float32)
    for s in range(COLS):
        c = 7 * (s // 8) + s % 8
        if c < 224:
            fold[s, c] = 1.0
    w256 += [fold.astype(ml_dtypes.bfloat16), fold.T.astype(ml_dtypes.bfloat16)]
    w256 += halves(mode_table())
    w128 += halves(np.kron(np.eye(EZ, dtype=np.float32), derivative))
    w128 += halves(np.kron(np.eye(EZ, dtype=np.float32), stiffness))
    first, second = row_maps()
    ra_a, ra_b, ea_a, ea_b = (np.zeros((ROWS, ROWS), np.float32) for _ in range(4))
    for packed, fold_rows, unfold_rows in ((first, ra_a, ea_a), (second, ra_b, ea_b)):
        for at, (e, j) in packed.items():
            fold_rows[at, 8 * e + j] = 1.0
            if j == 0 and e > 0:
                fold_rows[at, 8 * e - 1] = 1.0
            unfold_rows[:, at] = fold_rows[at]
    ea_a[ROWS - 1, UNIQUE] = 1.0
    ea_b[ROWS - 1, 14] = 1.0
    w128 += [m.astype(ml_dtypes.bfloat16) for m in (ra_a, ra_b, ea_a, ea_b)]
    weight_a = np.tile(weights, EZ)[:, None] * np.ones((1, COLS), np.float32)
    weight_r = np.tile(weights, 32)[None, :] * np.ones((ROWS, 1), np.float32)
    a, r = np.arange(ROWS), np.arange(COLS)
    count_a = np.where((a % 8 == 0) | (a % 8 == 7), 2.0, 1.0)
    count_r = np.where(((r % 8 == 7) & (r < 255)) | ((r % 8 == 0) & (r > 0)), 2.0, 1.0)
    inner = 1.0 / (count_a[:, None] * count_r[None, :])
    nodes = np.stack([weight_a, weight_r, inner]).astype(np.float32)
    return np.stack(w256), np.stack(w128), nodes, stiffness


def split(x):
    high = x.astype(BF16)
    return high, (x - high.astype(F32)).astype(BF16)


def dot(a, b):
    return jnp.dot(a, b, preferred_element_type=F32)


def left3(high, low, x):
    xh, xl = split(x)
    return dot(high, xh) + dot(high, xl) + dot(low, xh)


def right3(x, high, low):
    xh, xl = split(x)
    return dot(xh, high) + dot(xl, high) + dot(xh, low)


def left2(matrix, x):
    xh, xl = split(x)
    return dot(matrix, xh) + dot(matrix, xl)


def right2(x, matrix):
    xh, xl = split(x)
    return dot(xh, matrix) + dot(xl, matrix)


def roll(x, shift, axis):
    size = x.shape[axis]
    shift %= size
    return pltpu.roll(x, shift, axis) if shift else x


def lanes(shape):
    return lax.broadcasted_iota(jnp.int32, shape, 1)


def sublanes(shape):
    return lax.broadcasted_iota(jnp.int32, shape, 0)


def join_cols(field):
    lane = lanes(field.shape)
    total = (
        field
        + jnp.where((lane % 8 == 7), roll(field, -1, 1), 0.0)
        + jnp.where((lane % 8 == 0) & (lane > 0), roll(field, 1, 1), 0.0)
    )
    return jnp.where(lane == COLS - 1, 0.0, total)


def join_rows(field):
    row = sublanes(field.shape)
    return (
        field
        + jnp.where((row % 8 == 7) & (row < ROWS - 1), roll(field, -1, 0), 0.0)
        + jnp.where((row % 8 == 0) & (row > 0), roll(field, 1, 0), 0.0)
    )


def make_kernel(stiffness):
    def kernel(
        va_hbm,
        vr_hbm,
        ax_hbm,
        ma_hbm,
        mr_hbm,
        w256_hbm,
        w128_hbm,
        nodes_hbm,
        out_ref,
        va,
        vr,
        ax,
        ma_s,
        mr_s,
        w256,
        w128,
        nodes,
        metric,
        mass,
        coef,
        packed_a,
        packed_b,
        send1,
        recv1,
        send2,
        recv2,
        seam_s,
        seam_r,
        edge_s,
        edge_r,
        b_s,
        v_s,
        mrow,
        mom_s,
        mom_r,
        in_sem,
        s1,
        r1,
        s2,
        r2,
        hs,
        hr,
        ms,
        mr_sem,
    ):
        me = lax.axis_index("fourier")
        z = lax.axis_index("elem")
        up, down = lax.rem(z + 1, NZ), lax.rem(z + NZ - 1, NZ)

        loads = [
            pltpu.make_async_copy(src, dst, in_sem.at[i])
            for i, (src, dst) in enumerate(
                (
                    (ma_hbm, ma_s),
                    (mr_hbm, mr_s),
                    (nodes_hbm, nodes),
                    (w128_hbm, w128),
                    (ax_hbm, ax),
                    (w256_hbm, w256),
                    (va_hbm, va),
                    (vr_hbm, vr),
                )
            )
        ]
        for load in loads:
            load.start()

        barrier = pltpu.get_barrier_semaphore()

        def greet_f(k, carry):
            pl.semaphore_signal(
                barrier, inc=1, device_id=(lax.rem(me + k, NF), z), device_id_type=MESH
            )
            return carry

        def greet_z(k, carry):
            pl.semaphore_signal(
                barrier, inc=1, device_id=(me, lax.rem(z + k, NZ)), device_id_type=MESH
            )
            return carry

        recv2[pl.ds(UNITS * 8, (PADDED - UNITS) * 8), :] = jnp.zeros(
            ((PADDED - UNITS) * 8, 128), F32
        )
        lax.fori_loop(1, NZ, greet_z, 0)
        lax.fori_loop(1, NF, greet_f, 0)

        for load in loads[:3]:
            load.wait()
        up_rows = (lanes((ROWS, EZ)) == sublanes((ROWS, EZ)) // 8).astype(F32)
        up_cols = (sublanes((32, COLS)) == lanes((32, COLS)) // 8).astype(F32)

        def widen(values):
            tall = jnp.dot(up_rows, values, precision=HIGH, preferred_element_type=F32)
            return jnp.dot(tall, up_cols, precision=HIGH, preferred_element_type=F32)

        metric_a = widen(ma_s[...])
        metric_r = widen(mr_s[...])
        weight_a, weight_r = nodes[0], nodes[1]
        metric[0] = metric_a
        metric[1] = metric_r
        mass[...] = weight_a * weight_r / (metric_a * metric_r)
        coef[0] = metric_a / metric_r * weight_r
        coef[1] = metric_r / metric_a * weight_a

        for load in loads[3:]:
            load.wait()

        def drive_plane(p, carry):
            x = ax[p]
            xh, xl = split(x)
            grad_a = dot(w128[DA_H], xh) + dot(w128[DA_H], xl) + dot(w128[DA_L], xh)
            grad_r = dot(xh, w256[DR_H]) + dot(xl, w256[DR_H]) + dot(xh, w256[DR_L])
            nonlinear = va[p] * (grad_a * metric[0]) + vr[p] * (grad_r * metric[1])
            loaded = (2.0 * x - nonlinear) * 2.0 * mass[...]
            folded = right2(loaded, w256[SR])
            b_s[p] = folded
            high, low = split(folded)
            packed_a[p] = dot(w128[RA_A], high[:, :128]) + dot(w128[RA_A], low[:, :128])
            packed_b[p] = dot(w128[RA_B], high[:, 128:]) + dot(w128[RA_B], low[:, 128:])
            return carry

        lax.fori_loop(0, 4, drive_plane, 0)

        lane128 = lanes((16, 128))
        for p in range(4):
            seam_s[2 * p : 2 * p + 1, :] = b_s[p, 0:1, :]
            seam_s[2 * p + 1 : 2 * p + 2, :] = b_s[p, ROWS - 1 : ROWS, :]
            for h in range(2):
                send1[pl.ds(2 * p + h, A_UNITS, stride=8), :] = packed_a[
                    p, h * A_UNITS : (h + 1) * A_UNITS, :
                ]
                quarters = [
                    packed_b[p, (4 * h + q) * 16 : (4 * h + q + 1) * 16, :] for q in range(4)
                ]
                for t in range(3):
                    tile = roll(quarters[0], -32 * t, 1)
                    for q in range(1, 4):
                        tile = jnp.where(lane128 >= 32 * q, roll(quarters[q], 32 * (q - t), 1), tile)
                    send1[pl.ds((B_BASE + t) * 8 + 2 * p + h, 16, stride=24), :] = tile

        pl.semaphore_wait(barrier, NF - 1 + NZ - 1)

        def exchange(src, dst, at):
            copies = [
                pltpu.make_async_remote_copy(
                    src_ref=src,
                    dst_ref=dst.at[side],
                    send_sem=hs.at[at + side],
                    recv_sem=hr.at[at + side],
                    device_id=(me, target),
                    device_id_type=MESH,
                )
                for side, target in ((0, up), (1, down))
            ]
            for copy in copies:
                copy.start()
            return copies

        seam = exchange(seam_s, seam_r, 0)

        def tile_at(index):
            return pl.ds(pl.multiple_of(index * 8, 8), 8)

        def send_plane(unit, slot, target):
            pltpu.make_async_remote_copy(
                src_ref=send1.at[tile_at(unit), :],
                dst_ref=recv1.at[slot, tile_at(me), :],
                send_sem=s1.at[slot],
                recv_sem=r1.at[slot],
                device_id=(target, z),
                device_id_type=MESH,
            ).start()

        def first_chunk(k, carry):
            target = lax.rem(me + k, NF)
            waits = target == 0
            for unit in SEAM[1:]:
                waits = waits | (target == unit)

            @pl.when(jnp.logical_not(waits))
            def _():
                send_plane(target, 0, target)

            return carry

        lax.fori_loop(1, NF, first_chunk, 0)

        for copy in seam:
            copy.wait()
        own = seam_s[...]
        below, above = seam_r[0], seam_r[1]
        even = sublanes((8, 128)) % 2 == 0
        add_a = roll(below[:, :128], -1, 0)
        add_b = roll(below[:, 128:], -1, 0)
        lane = lanes((8, 128))
        send1[0:8, :] = send1[0:8, :] + jnp.where(even, add_a, 0.0)
        for t in range(3):
            at = (B_BASE + t) * 8
            send1[at : at + 8, :] = send1[at : at + 8, :] + jnp.where(
                even & (lane < 32), roll(add_b, -32 * t, 1), 0.0
            )
        top_a = roll(own[:, :128], -1, 0) + above[:, :128]
        top_b = own[:, 128:] + roll(above[:, 128:], 1, 0)
        send1[X_UNIT * 8 : X_UNIT * 8 + 8, :] = jnp.where(even, top_a, top_b)

        for unit in SEAM:

            @pl.when(me != unit)
            def _(unit=unit):
                send_plane(unit, 0, unit)

        def second_chunk(k, carry):
            chip = lax.rem(me // 2 + k, NF // 2)

            @pl.when(2 * chip != me)
            def _():
                send_plane(FIRST + chip, 1, 2 * chip)

            return carry

        lax.fori_loop(0, NF // 2, second_chunk, 0)
        for at, target in enumerate(EXTRA):

            @pl.when(me != target)
            def _(at=at, target=target):
                send_plane(FIRST + NF // 2 + at, 1, target)

        unit1 = FIRST + me // 2
        owner1 = me % 2 == 0
        for at, target in enumerate(EXTRA):
            unit1 = jnp.where(me == target, FIRST + NF // 2 + at, unit1)
            owner1 = owner1 | (me == target)

        recv1[0, tile_at(me), :] = send1[tile_at(me), :]

        def await_tiles(ref, count, sem):
            view = ref.at[pl.ds(0, count * 8), :]
            pltpu.make_async_copy(view, view, sem).wait()

        def transform(slot, unit):
            x = jnp.concatenate(
                [recv1[slot, pl.ds(h, PLANES, stride=2), :] for h in range(2)], axis=1
            )
            y = left3(w256[C_H], w256[C_L], x)
            for h in range(2):
                send2[slot, pl.ds(h, PLANES, stride=2), :] = y[:, 128 * h : 128 * (h + 1)]

            def send_modes(k, carry):
                target = lax.rem(me + k, NF)
                pltpu.make_async_remote_copy(
                    src_ref=send2.at[slot, tile_at(target), :],
                    dst_ref=recv2.at[tile_at(unit), :],
                    send_sem=s2.at[slot],
                    recv_sem=r2.at[slot],
                    device_id=(target, z),
                    device_id_type=MESH,
                ).start()
                return carry

            lax.fori_loop(1, NF, send_modes, 0)
            recv2[tile_at(unit), :] = send2[slot, tile_at(me), :]

        await_tiles(recv1.at[0], NF - 1, r1.at[0])
        transform(0, me)

        @pl.when(owner1)
        def _():
            recv1[1, tile_at(me), :] = send1[tile_at(unit1), :]
            await_tiles(recv1.at[1], NF - 1, r1.at[1])
            transform(1, unit1)

        await_tiles(recv2, NF - 1, r2.at[0])
        sub = sublanes((8, COLS))
        low_side = sub % 2 == 0
        x_tile = recv2[X_UNIT * 8 : X_UNIT * 8 + 8, :]
        edge_rows = []
        for j in range(8):
            g, q = j // 4, j % 4
            part_a = recv2[8 * j : 8 * j + 8, :]
            pieces = [
                recv2[(B_BASE + 3 * g + t) * 8 : (B_BASE + 3 * g + t) * 8 + 8, :] for t in range(3)
            ]
            part_b = roll(pieces[0], -32 * q, 1)
            for t in range(1, 3):
                part_b = jnp.where(lane >= 32 * t, roll(pieces[t], 32 * (t - q), 1), part_b)
            if j == 7:
                part_a = jnp.where(even, part_a, roll(x_tile, 1, 0))
                part_b = jnp.where(even, part_b, x_tile)
            edge_rows.append(jnp.concatenate([part_a, part_b], axis=1))
        edge = right2(jnp.concatenate(edge_rows, axis=0), w256[ER])
        along_a = jnp.zeros((8, COLS), F32)
        for j in range(8):
            factor = jnp.where(low_side, float(stiffness[0, j]), float(stiffness[7, j]))
            along_a = along_a + factor * edge[8 * j : 8 * j + 8]
        chosen = jnp.where(low_side, edge[0:8], edge[56:64])
        along_r = right3(chosen, w256[KR_H], w256[KR_L])

        def edge_coef(ref):
            return jnp.where(low_side, ref[0:1, :], ref[ROWS - 1 : ROWS, :])

        def shift_of(mode):
            wave = jnp.where(mode == 1, PLANES // 2, mode // 2)
            return 4.0 + (wave.astype(F32) * 0.03125) * (wave.astype(F32) * 0.03125)

        edge_shift = shift_of(4 * me + sub // 2)
        image = (
            edge_coef(coef.at[0]) * along_a
            + edge_coef(coef.at[1]) * along_r
            + edge_shift * edge_coef(mass) * chosen
        )
        edge_s[...] = join_cols(image)
        edges = exchange(edge_s, edge_r, 2)

        for p in range(4):
            for h in range(2):
                packed_a[p, h * A_UNITS : (h + 1) * A_UNITS, :] = recv2[
                    pl.ds(2 * p + h, A_UNITS, stride=8), :
                ]
            packed_a[p, UNIQUE : UNIQUE + 8, :] = jnp.where(
                sublanes((8, 128)) == 0, x_tile[2 * p : 2 * p + 1, :], 0.0
            )
            packed_a[p, UNIQUE + 8 : ROWS, :] = jnp.zeros((8, 128), F32)

        for copy in edges:
            copy.wait()

        @pl.when(owner1)
        def _():
            await_tiles(recv2, UNITS - FIRST - 1, r2.at[1])

        @pl.when(jnp.logical_not(owner1))
        def _():
            await_tiles(recv2, UNITS - FIRST, r2.at[1])

        for p in range(4):
            for h in range(2):
                pieces = [
                    recv2[pl.ds((B_BASE + t) * 8 + 2 * p + h, 16, stride=24), :] for t in range(3)
                ]
                for q in range(4):
                    part_b = roll(pieces[0], -32 * q, 1)
                    for t in range(1, 3):
                        part_b = jnp.where(
                            lane128 >= 32 * t, roll(pieces[t], 32 * (t - q), 1), part_b
                        )
                    if h == 0 and q == 0:
                        part_b = jnp.where(
                            sublanes((16, 128)) == 14, x_tile[2 * p + 1 : 2 * p + 2, :], part_b
                        )
                    packed_b[p, (4 * h + q) * 16 : (4 * h + q + 1) * 16, :] = part_b

        def operate(field, shift):
            high, low = split(field)
            along_a = dot(w128[KA_H], high) + dot(w128[KA_H], low) + dot(w128[KA_L], high)
            along_r = dot(high, w256[KR_H]) + dot(low, w256[KR_H]) + dot(high, w256[KR_L])
            return along_a * coef[0] + along_r * coef[1] + shift * mass[...] * field

        def total(field):
            row = jnp.sum(field, axis=0, keepdims=True)
            return row[:, :128] + row[:, 128:]

        row_ids = sublanes((ROWS, COLS))

        def mode_step(p, carry):
            wide = jnp.concatenate(
                [left2(w128[EA_A], packed_a[p]), left2(w128[EA_B], packed_b[p])], axis=1
            )
            right = right2(wide, w256[ER])
            shift = shift_of(4 * me + p)
            raw = operate(right, shift)
            joined = join_rows(join_cols(raw))
            from_below = edge_r[0, pl.ds(2 * p + 1, 1), :]
            from_above = edge_r[1, pl.ds(2 * p, 1), :]
            joined = (
                joined
                + jnp.where(row_ids == 0, from_below, 0.0)
                + jnp.where(row_ids == ROWS - 1, from_above, 0.0)
            )
            raw2 = operate(joined, shift)
            inner = nodes[2]
            b_s[p] = right
            v_s[p] = joined
            mrow[p] = jnp.concatenate(
                [
                    total(inner * right * right),
                    total(right * raw),
                    total(inner * joined * joined),
                    total(joined * raw2),
                    jnp.zeros((4, 128), F32),
                ],
                axis=0,
            )
            return carry

        lax.fori_loop(0, 4, mode_step, 0)

        sums = jnp.sum(
            jnp.concatenate([mrow[p] for p in range(4)], axis=0), axis=1, keepdims=True
        )
        row32, lane32 = sublanes((32, 128)), lanes((32, 128))
        mine = (row32 % 8 < 4) & (lane32 // 8 == (row32 // 8) * 4 + row32 % 8)
        moments = jnp.sum(jnp.where(mine, sums, 0.0), axis=0, keepdims=True)
        mom_s[...] = moments
        mom_r[z] = moments

        def send_moments(k, carry):
            pltpu.make_async_remote_copy(
                src_ref=mom_s,
                dst_ref=mom_r.at[z],
                send_sem=ms,
                recv_sem=mr_sem,
                device_id=(me, lax.rem(z + k, NZ)),
                device_id_type=MESH,
            ).start()
            return carry

        lax.fori_loop(1, NZ, send_moments, 0)
        view = mom_r.at[pl.ds(0, NZ - 1)]
        pltpu.make_async_copy(view, view, mr_sem).wait()
        pooled = mom_r[0]
        for at in range(1, NZ):
            pooled = pooled + mom_r[at]
        m0 = pooled
        m1, m2, m3 = (roll(pooled, -8 * k, 1) for k in range(1, 4))
        alpha0 = m0 / m1
        norm1 = alpha0 * alpha0 * m2 - m0
        gain = 1.0 + norm1 / m0
        curve = gain * gain * m1 - 2.0 * gain * alpha0 * m2 + alpha0 * alpha0 * m3
        alpha1 = norm1 / curve
        on_right = alpha0 + alpha1 * gain
        on_image = -alpha1 * alpha0
        lane1 = lanes((1, 128))
        for p in range(4):
            pick = lane1 == 32 * p
            first = jnp.sum(jnp.where(pick, on_right, 0.0), axis=1, keepdims=True)
            second = jnp.sum(jnp.where(pick, on_image, 0.0), axis=1, keepdims=True)
            out_ref[p] = first * b_s[p] + second * v_s[p]

        pltpu.make_async_copy(view, view, ms).wait()
        await_tiles(recv1.at[0], NF - 1, s1.at[0])
        await_tiles(recv2, NF - 1, s2.at[0])

        @pl.when(owner1)
        def _():
            await_tiles(recv1.at[1], UNITS - FIRST - 1, s1.at[1])
            await_tiles(recv2, NF - 1, s2.at[1])

        @pl.when(jnp.logical_not(owner1))
        def _():
            await_tiles(recv1.at[1], UNITS - FIRST, s1.at[1])

    return kernel


def solution(mesh):
    w256, w128, nodes, stiffness = tables()
    kernel = make_kernel(stiffness)

    def shards(vel_az, vel_rad, axial, metric_az, metric_rad):
        field = (4, ROWS, COLS)
        return pl.pallas_call(
            kernel,
            out_shape=jax.ShapeDtypeStruct(field, F32),
            in_specs=[pl.BlockSpec(memory_space=pltpu.HBM)] * 8,
            out_specs=pl.BlockSpec(memory_space=pltpu.VMEM),
            scratch_shapes=[
                pltpu.VMEM(field, F32),
                pltpu.VMEM(field, F32),
                pltpu.VMEM(field, F32),
                pltpu.VMEM((EZ, 32), F32),
                pltpu.VMEM((EZ, 32), F32),
                pltpu.VMEM(w256.shape, BF16),
                pltpu.VMEM(w128.shape, BF16),
                pltpu.VMEM(nodes.shape, F32),
                pltpu.VMEM((2, ROWS, COLS), F32),
                pltpu.VMEM((ROWS, COLS), F32),
                pltpu.VMEM((2, ROWS, COLS), F32),
                pltpu.VMEM((4, ROWS, 128), F32),
                pltpu.VMEM((4, ROWS, 128), F32),
                pltpu.VMEM((PADDED * 8, 128), F32),
                pltpu.VMEM((2, NF * 8, 128), F32),
                pltpu.VMEM((2, NF * 8, 128), F32),
                pltpu.VMEM((PADDED * 8, 128), F32),
                pltpu.VMEM((8, COLS), F32),
                pltpu.VMEM((2, 8, COLS), F32),
                pltpu.VMEM((8, COLS), F32),
                pltpu.VMEM((2, 8, COLS), F32),
                pltpu.VMEM(field, F32),
                pltpu.VMEM(field, F32),
                pltpu.VMEM((4, 8, 128), F32),
                pltpu.VMEM((1, 128), F32),
                pltpu.VMEM((NZ, 1, 128), F32),
                pltpu.SemaphoreType.DMA((8,)),
                pltpu.SemaphoreType.DMA((2,)),
                pltpu.SemaphoreType.DMA((2,)),
                pltpu.SemaphoreType.DMA((2,)),
                pltpu.SemaphoreType.DMA((2,)),
                pltpu.SemaphoreType.DMA((4,)),
                pltpu.SemaphoreType.DMA((4,)),
                pltpu.SemaphoreType.DMA(()),
                pltpu.SemaphoreType.DMA(()),
            ],
            compiler_params=pltpu.CompilerParams(
                collective_id=0, has_side_effects=True, vmem_limit_bytes=56 * 2**20
            ),
        )(
            vel_az,
            vel_rad,
            axial,
            metric_az,
            metric_rad,
            jnp.asarray(w256),
            jnp.asarray(w128),
            jnp.asarray(nodes),
        )

    spec = P("fourier", "elem", None)
    metric_spec = P("elem", None)
    return jax.shard_map(
        shards,
        mesh=mesh,
        in_specs=(spec, spec, spec, metric_spec, metric_spec),
        out_specs=spec,
        check_vma=False,
    )
```

```python
import math

import jax
import jax.numpy as jnp
import ml_dtypes
import numpy as np
from jax import lax
from jax.experimental import pallas as pl
from jax.experimental.pallas import tpu as pltpu
from jax.sharding import PartitionSpec as P

MESH = pl.DeviceIdType.MESH
F32 = jnp.float32
BF16 = jnp.bfloat16
HIGH = lax.Precision.HIGHEST

PLANES = 256
NODES = 8
NF = 64
NZ = 16
ROWS = 128
COLS = 256
EZ = 16
UNIQUE = 7 * EZ
A_UNITS = 56
X_UNIT = 56
B_BASE = 57
UNITS = 99
PADDED = 105
FIRST = 64
EXTRA = (1, 27, 45)

DR_H, DR_L, SR, KR_H, KR_L, ER, C_H, C_L = range(8)
RA_B, EA_B = range(2)


def gll_tables():
    points = np.array(
        [
            -1.0,
            -0.8717401485096066,
            -0.5917001814331423,
            -0.2092992179024789,
            0.2092992179024789,
            0.5917001814331423,
            0.8717401485096066,
            1.0,
        ]
    )
    gll_weights = np.array(
        [
            0.03571428571428571,
            0.2107042271435061,
            0.3411226924835044,
            0.4124587946587038,
            0.4124587946587038,
            0.3411226924835044,
            0.2107042271435061,
            0.03571428571428571,
        ]
    )
    number = points.shape[0]
    scales = np.array(
        [
            np.prod([points[col_at] - points[other] for other in range(number) if other != col_at])
            for col_at in range(number)
        ]
    )
    derivative = np.zeros((number, number))
    for row_at in range(number):
        for col_at in range(number):
            if row_at != col_at:
                derivative[row_at, col_at] = scales[row_at] / (
                    scales[col_at] * (points[row_at] - points[col_at])
                )
    for row_at in range(number):
        derivative[row_at, row_at] = -np.sum(derivative[row_at])
    stiffness = derivative.T @ (gll_weights[:, None] * derivative)
    return (
        gll_weights.astype(np.float32),
        derivative.astype(np.float32),
        stiffness.astype(np.float32),
    )


def mode_table():
    modes = np.arange(PLANES)
    waves = np.where(modes == 1, PLANES // 2, modes // 2)
    phase = waves[:, None] * np.arange(PLANES)[None, :] % PLANES
    angles = phase * (2.0 * math.pi / PLANES)
    odd = (modes % 2 == 1) & (modes > 1)
    return (np.where(odd[:, None], -np.sin(angles), np.cos(angles)) / math.sqrt(PLANES)).astype(
        np.float32
    )


def halves(matrix):
    high = matrix.astype(ml_dtypes.bfloat16)
    low = (matrix - high.astype(np.float32)).astype(ml_dtypes.bfloat16)
    return [high, low]


def row_map():
    every = [(e, j) for e in range(EZ) for j in range(7)]
    second = {}
    for g in range(2):
        for q in range(4):
            j = g * 4 + q
            second[q * 16 + g] = (0, j) if j < 7 else (1, 0)
            if j < 7:
                second[(4 + q) * 16 + g] = (EZ - 1, j)
    left = [r for r in every if r not in second.values()]
    for block in range(8):
        for g in range(14):
            if block * 16 + g not in second:
                second[block * 16 + g] = left.pop(0)
    return second


def tables():
    weights, derivative, stiffness = gll_tables()
    w256 = halves(np.kron(np.eye(32, dtype=np.float32), derivative).T)
    fold = np.zeros((COLS, COLS), np.float32)
    for s in range(COLS):
        c = 7 * (s // 8) + s % 8
        if c < 224:
            fold[s, c] = 1.0
    w256 += [fold.astype(ml_dtypes.bfloat16)]
    w256 += halves(np.kron(np.eye(32, dtype=np.float32), stiffness).T)
    w256 += [fold.T.astype(ml_dtypes.bfloat16)]
    w256 += halves(mode_table())
    fold_rows = np.zeros((ROWS, ROWS), np.float32)
    for at, (e, j) in row_map().items():
        fold_rows[at, j * EZ + e] = 1.0
        if j == 0 and e > 0:
            fold_rows[at, 7 * EZ + e - 1] = 1.0
    unfold_rows = fold_rows.T.copy()
    unfold_rows[ROWS - 1, 14] = 1.0
    w128 = [m.astype(ml_dtypes.bfloat16) for m in (fold_rows, unfold_rows)]
    return np.stack(w256), np.stack(w128), weights, derivative, stiffness


def split(x):
    high = x.astype(BF16)
    return high, (x - high.astype(F32)).astype(BF16)


def dot(a, b):
    return jnp.dot(a, b, preferred_element_type=F32)


def left3(high, low, x):
    xh, xl = split(x)
    return dot(high, xh) + dot(high, xl) + dot(low, xh)


def right3(x, high, low):
    xh, xl = split(x)
    return dot(xh, high) + dot(xl, high) + dot(xh, low)


def right2(x, matrix):
    xh, xl = split(x)
    return dot(xh, matrix) + dot(xl, matrix)


def roll(x, shift, axis):
    size = x.shape[axis]
    shift %= size
    return pltpu.roll(x, shift, axis) if shift else x


def lanes(shape):
    return lax.broadcasted_iota(jnp.int32, shape, 1)


def sublanes(shape):
    return lax.broadcasted_iota(jnp.int32, shape, 0)


def join_cols(field):
    lane = lanes(field.shape)
    total = (
        field
        + jnp.where((lane % 8 == 7), roll(field, -1, 1), 0.0)
        + jnp.where((lane % 8 == 0) & (lane > 0), roll(field, 1, 1), 0.0)
    )
    return jnp.where(lane == COLS - 1, 0.0, total)


def along(matrix, slabs, j):
    total = float(matrix[j, 0]) * slabs[0]
    for i in range(1, NODES):
        total = total + float(matrix[j, i]) * slabs[i]
    return total


def make_kernel(weights, derivative, stiffness):
    def kernel(
        va_hbm,
        vr_hbm,
        ax_hbm,
        ma_hbm,
        mr_hbm,
        w256_hbm,
        w128_hbm,
        b_s,
        v_s,
        factors,
        va,
        vr,
        ax,
        ma_s,
        mr_s,
        w256,
        w128,
        metric,
        x_s,
        packed_b,
        send1,
        recv1,
        send2,
        recv2,
        meet_s,
        meet_r,
        edge_s,
        edge_r,
        edge_image,
        edge_right,
        mrow,
        mom_s,
        mom_r,
        in_sem,
        s1,
        r1,
        s2,
        r2,
        hs,
        hr,
        ms,
        mr_sem,
    ):
        me = lax.axis_index("fourier")
        z = lax.axis_index("elem")
        up, down = lax.rem(z + 1, NZ), lax.rem(z + NZ - 1, NZ)

        barrier = pltpu.get_barrier_semaphore()

        def far_first(k, size):
            step = (k + 1) // 2
            return size // 2 + step * (1 - 2 * lax.rem(k, 2))

        def peer_f(k):
            row, col, core = me // 8, lax.rem(me // 2, 4), lax.rem(me, 2)
            row = lax.rem(row + far_first(k // 8, 8), 8)
            col = lax.rem(col + far_first(lax.rem(k // 2, 4), 4), 4)
            core = lax.rem(core + 1 + lax.rem(k, 2), 2)
            return row * 8 + col * 2 + core

        def peer_z(k):
            return lax.rem(z + far_first(k, NZ), NZ)

        def greet_f(k, carry):
            pl.semaphore_signal(barrier, inc=1, device_id=(peer_f(k), z), device_id_type=MESH)
            return carry

        def greet_z(k, carry):
            pl.semaphore_signal(barrier, inc=1, device_id=(me, peer_z(k)), device_id_type=MESH)
            return carry

        lax.fori_loop(0, NZ - 1, greet_z, 0, unroll=True)
        lax.fori_loop(0, NF - 1, greet_f, 0, unroll=True)

        loads = [
            pltpu.make_async_copy(src, dst, in_sem.at[i])
            for i, (src, dst) in enumerate(
                [(ma_hbm, ma_s), (mr_hbm, mr_s)]
                + [(ref.at[p, :, pl.ds(128 * h, 128)], to.at[p, h]) for p in range(4) for ref, to in ((ax_hbm, ax), (va_hbm, va), (vr_hbm, vr)) for h in range(2)]
                + [(w256_hbm.at[pl.ds(0, KR_H)], w256.at[pl.ds(0, KR_H)]), (w128_hbm, w128)]
            )
        ]
        late = pltpu.make_async_copy(
            w256_hbm.at[pl.ds(KR_H, 8 - KR_H)], w256.at[pl.ds(KR_H, 8 - KR_H)], in_sem.at[28]
        )
        for load in loads:
            load.start()
        recv2[pl.ds(UNITS * 8, (PADDED - UNITS) * 8), :] = jnp.zeros(
            ((PADDED - UNITS) * 8, 128), F32
        )

        for load in loads[:2]:
            load.wait()
        up_cols = (sublanes((32, COLS)) == lanes((32, COLS)) // 8).astype(F32)
        wide = jnp.dot(
            jnp.concatenate([ma_s[...], mr_s[...]], axis=0),
            up_cols,
            precision=HIGH,
            preferred_element_type=F32,
        )
        metric_a, metric_r = wide[:EZ], wide[EZ:]

        def end_weights(shape):
            place = lanes(shape) % 8
            place = jnp.minimum(place, 7 - place)
            value = jnp.full(shape, float(weights[3]), F32)
            for at in range(3):
                value = jnp.where(place == at, float(weights[at]), value)
            return value

        weight_r = end_weights((1, COLS))
        metric[0] = metric_a
        metric[1] = metric_r
        metric[2] = weight_r / (metric_a * metric_r)
        metric[3] = metric_a / metric_r * weight_r
        metric[4] = metric_r / metric_a
        meet_s[...] = jnp.zeros((8, COLS), F32)
        for row, values in enumerate((metric_a, metric_r)):
            meet_s[2 * row : 2 * row + 1, :] = values[0:1]
            meet_s[2 * row + 1 : 2 * row + 2, :] = values[EZ - 1 :]

        for load in loads[26:]:
            load.wait()

        lane128 = lanes((16, 128))

        row16 = sublanes((EZ, COLS))
        for p in range(4):
            for load in loads[2 + 6 * p : 8 + 6 * p]:
                load.wait()

            def slab_of(ref, j, p=p):
                return jnp.concatenate(
                    [ref[p, h, pl.ds(j, EZ, stride=8), :] for h in range(2)], axis=1
                )

            slabs = [slab_of(ax, j) for j in range(NODES)]
            for j in range(NODES):
                x_s[j * EZ : (j + 1) * EZ, :] = slabs[j]
            x_all = x_s[...]
            grad_r = right3(x_all, w256[DR_H], w256[DR_L])
            loaded = []
            for j in range(NODES):
                grad_a = along(derivative, slabs, j)
                nonlinear = slab_of(va, j) * (grad_a * metric[0]) + slab_of(vr, j) * (
                    grad_r[j * EZ : (j + 1) * EZ] * metric[1]
                )
                loaded.append(
                    (2.0 * slabs[j] - nonlinear) * ((2.0 * float(weights[j])) * metric[2])
                )
            folded = right2(jnp.concatenate(loaded, axis=0), w256[SR])
            last = folded[ROWS - 1 :]
            for h in range(2):
                send1[X_UNIT * 8 + 2 * p + h : X_UNIT * 8 + 2 * p + h + 1, :] = last[
                    :, 128 * h : 128 * h + 128
                ]
            start = folded[:EZ, :128] + jnp.where(
                row16[:, :128] > 0, roll(folded[7 * EZ :, :128], 1, 0), 0.0
            )
            for j in range(7):
                slab = start if j == 0 else folded[j * EZ : (j + 1) * EZ, :128]
                for h in range(2):
                    send1[pl.ds(64 * j + 2 * p + h, 8, stride=8), :] = slab[8 * h : 8 * h + 8]
            high, low = split(folded[:, 128:])
            packed = dot(w128[RA_B], high) + dot(w128[RA_B], low)
            for h in range(2):
                quarters = [packed[(4 * h + q) * 16 : (4 * h + q + 1) * 16] for q in range(4)]
                for t in range(3):
                    tile = roll(quarters[0], -32 * t, 1)
                    for q in range(1, 4):
                        tile = jnp.where(lane128 >= 32 * q, roll(quarters[q], 32 * (q - t), 1), tile)
                    send1[pl.ds((B_BASE + t) * 8 + 2 * p + h, 16, stride=24), :] = tile
        late.start()

        pl.semaphore_wait(barrier, NF - 1 + NZ - 1)

        def exchange(src, dst, at):
            copies = [
                pltpu.make_async_remote_copy(
                    src_ref=src,
                    dst_ref=dst.at[side],
                    send_sem=hs.at[at + side],
                    recv_sem=hr.at[at + side],
                    device_id=(me, target),
                    device_id_type=MESH,
                )
                for side, target in ((0, up), (1, down))
            ]
            for copy in copies:
                copy.start()
            return copies

        def tile_at(index):
            return pl.ds(pl.multiple_of(index * 8, 8), 8)

        def send_plane(unit, slot, target):
            pltpu.make_async_remote_copy(
                src_ref=send1.at[tile_at(unit), :],
                dst_ref=recv1.at[slot, tile_at(me), :],
                send_sem=s1.at[slot],
                recv_sem=r1.at[slot],
                device_id=(target, z),
                device_id_type=MESH,
            ).start()

        def first_chunk(k, carry):
            target = peer_f(k)
            send_plane(target, 0, target)
            return carry

        def second_chunk(k, carry):
            row = lax.rem(me // 8 + far_first(k // 4, 8), 8)
            col = lax.rem(me // 2 + far_first(lax.rem(k, 4), 4), 4)
            chip = row * 4 + col

            @pl.when(2 * chip != me)
            def _():
                send_plane(FIRST + chip, 1, 2 * chip)

            return carry

        for at, target in enumerate(EXTRA):

            @pl.when(me != target)
            def _(at=at, target=target):
                send_plane(FIRST + NF // 2 + at, 1, target)

        lax.fori_loop(0, NF - 1, first_chunk, 0, unroll=True)
        meets = exchange(meet_s, meet_r, 0)
        lax.fori_loop(0, NF // 2, second_chunk, 0, unroll=True)
        unit1 = FIRST + me // 2
        owner1 = me % 2 == 0
        for at, target in enumerate(EXTRA):
            unit1 = jnp.where(me == target, FIRST + NF // 2 + at, unit1)
            owner1 = owner1 | (me == target)

        recv1[0, tile_at(me), :] = send1[tile_at(me), :]

        def await_tiles(ref, count, sem):
            view = ref.at[pl.ds(0, count * 8), :]
            pltpu.make_async_copy(view, view, sem).wait()

        def transform(slot, unit):
            x = jnp.concatenate(
                [recv1[slot, pl.ds(h, PLANES, stride=2), :] for h in range(2)], axis=1
            )
            y = left3(w256[C_H], w256[C_L], x)
            for h in range(2):
                send2[slot, pl.ds(h, PLANES, stride=2), :] = y[:, 128 * h : 128 * (h + 1)]

            def send_modes(k, carry):
                target = peer_f(k)
                pltpu.make_async_remote_copy(
                    src_ref=send2.at[slot, tile_at(target), :],
                    dst_ref=recv2.at[tile_at(unit), :],
                    send_sem=s2.at[slot],
                    recv_sem=r2.at[slot],
                    device_id=(target, z),
                    device_id_type=MESH,
                ).start()
                return carry

            lax.fori_loop(0, NF - 1, send_modes, 0, unroll=True)
            recv2[tile_at(unit), :] = send2[slot, tile_at(me), :]

        late.wait()
        await_tiles(recv1.at[0], NF - 1, r1.at[0])
        transform(0, me)

        @pl.when(owner1)
        def _():
            recv1[1, tile_at(me), :] = send1[tile_at(unit1), :]
            await_tiles(recv1.at[1], NF - 1, r1.at[1])
            transform(1, unit1)

        await_tiles(recv2, NF - 1, r2.at[0])
        even = sublanes((8, 128)) % 2 == 0
        lane = lanes((8, 128))
        sub = sublanes((8, COLS))
        low_side = sub % 2 == 0
        x_tile = recv2[X_UNIT * 8 : X_UNIT * 8 + 8, :]
        edge_rows = []
        for j in range(8):
            g, q = j // 4, j % 4
            start, end = (8 * j, 8 * j + 7) if j < 7 else (1, X_UNIT)
            part_a = jnp.where(
                even,
                recv2[8 * start : 8 * start + 8, :],
                recv2[8 * end : 8 * end + 8, :] if j < 7 else roll(x_tile, 1, 0),
            )
            pieces = [
                recv2[(B_BASE + 3 * g + t) * 8 : (B_BASE + 3 * g + t) * 8 + 8, :] for t in range(3)
            ]
            part_b = roll(pieces[0], -32 * q, 1)
            for t in range(1, 3):
                part_b = jnp.where(lane >= 32 * t, roll(pieces[t], 32 * (t - q), 1), part_b)
            if j == 7:
                part_b = jnp.where(even, part_b, x_tile)
            edge_rows.append(jnp.concatenate([part_a, part_b], axis=1))
        edge = right2(jnp.concatenate(edge_rows, axis=0), w256[ER])
        along_a = jnp.zeros((8, COLS), F32)
        for j in range(8):
            factor = jnp.where(low_side, float(stiffness[0, j]), float(stiffness[7, j]))
            along_a = along_a + factor * edge[8 * j : 8 * j + 8]
        chosen = jnp.where(low_side, edge[0:8], edge[56:64])
        along_r = right3(chosen, w256[KR_H], w256[KR_L])

        def edge_coef(at):
            return jnp.where(low_side, metric[at, 0:1, :], metric[at, EZ - 1 : EZ, :])

        def shift_of(mode):
            wave = jnp.where(mode == 1, PLANES // 2, mode // 2)
            return 4.0 + (wave.astype(F32) * 0.03125) * (wave.astype(F32) * 0.03125)

        edge_shift = shift_of(4 * me + sub // 2)
        end = float(weights[0])
        image = (
            edge_coef(3) * along_a
            + (end * edge_coef(4)) * along_r
            + edge_shift * (end * edge_coef(2)) * chosen
        )
        edge_s[0:8, :] = join_cols(image)
        edge_s[8:16, :] = chosen
        edges = exchange(edge_s, edge_r, 2)

        for copy in meets:
            copy.wait()
        next_a = jnp.where(low_side, meet_r[0, 1:2, :], meet_r[1, 0:1, :])
        next_r = jnp.where(low_side, meet_r[0, 3:4, :], meet_r[1, 2:3, :])
        corner = jnp.where(low_side, float(stiffness[7, 7]), float(stiffness[0, 0]))
        across = join_cols(
            next_a / next_r * weight_r * (corner * chosen)
            + (end * (next_r / next_a)) * along_r
            + edge_shift * (end * (weight_r / (next_a * next_r))) * chosen
        )

        for copy in edges:
            copy.wait()
        below, above = edge_r[0], edge_r[1]
        edge_image[...] = across + jnp.where(
            low_side, roll(below[0:8], -1, 0), roll(above[0:8], 1, 0)
        )
        edge_right[...] = jnp.where(low_side, roll(below[8:16], -1, 0), roll(above[8:16], 1, 0))

        @pl.when(owner1)
        def _():
            await_tiles(recv2, UNITS - FIRST - 1, r2.at[1])

        @pl.when(jnp.logical_not(owner1))
        def _():
            await_tiles(recv2, UNITS - FIRST, r2.at[1])

        for p in range(4):
            for h in range(2):
                pieces = [
                    recv2[pl.ds((B_BASE + t) * 8 + 2 * p + h, 16, stride=24), :] for t in range(3)
                ]
                for q in range(4):
                    part_b = roll(pieces[0], -32 * q, 1)
                    for t in range(1, 3):
                        part_b = jnp.where(
                            lane128 >= 32 * t, roll(pieces[t], 32 * (t - q), 1), part_b
                        )
                    if h == 0 and q == 0:
                        part_b = jnp.where(
                            sublanes((16, 128)) == 14, x_tile[2 * p + 1 : 2 * p + 2, :], part_b
                        )
                    packed_b[p, (4 * h + q) * 16 : (4 * h + q + 1) * 16, :] = part_b

        lane_r = lanes((1, COLS))
        inner_r = jnp.where(
            ((lane_r % 8 == 7) & (lane_r < COLS - 1)) | ((lane_r % 8 == 0) & (lane_r > 0)), 0.5, 1.0
        )

        def slabs_of(field):
            return [field[j * EZ : (j + 1) * EZ] for j in range(NODES)]

        def operate(field, shift):
            slabs = slabs_of(field)
            along_r = right3(field, w256[KR_H], w256[KR_L])
            heavy = shift * metric[2]
            return [
                metric[3] * along(stiffness, slabs, j)
                + float(weights[j])
                * (metric[4] * along_r[j * EZ : (j + 1) * EZ] + heavy * slabs[j])
                for j in range(NODES)
            ]

        def product(left, right, ends):
            total = ends * (left[0] * right[0] + left[7] * right[7])
            for j in range(1, 7):
                total = total + left[j] * right[j]
            return total

        def total(field):
            row = jnp.sum(field, axis=0, keepdims=True)
            return row[:, :128] + row[:, 128:]

        for p in range(4):
            left_cols = []
            for j in range(7):
                left_cols += [recv2[pl.ds(64 * j + 2 * p + h, 8, stride=8), :] for h in range(2)]
            first_slab = jnp.concatenate(left_cols[:2], axis=0)
            left_cols.append(
                jnp.where(
                    row16[:, :128] == EZ - 1, x_tile[2 * p : 2 * p + 1, :], roll(first_slab, -1, 0)
                )
            )
            high, low = split(packed_b[p])
            right_cols = dot(w128[EA_B], high) + dot(w128[EA_B], low)
            spread = right2(
                jnp.concatenate([jnp.concatenate(left_cols, axis=0), right_cols], axis=1), w256[ER]
            )
            x_s[...] = spread
            x_s[0:8, :] = spread[0:8] + jnp.where(
                sub == 0, edge_right[2 * p : 2 * p + 1, :], 0.0
            )
            x_s[ROWS - 8 :, :] = spread[ROWS - 8 :] + jnp.where(
                sub == 7, edge_right[2 * p + 1 : 2 * p + 2, :], 0.0
            )
            right = x_s[...]
            shift = shift_of(4 * me + p)
            raw = operate(right, shift)
            joined = join_cols(jnp.concatenate(raw, axis=0))
            low_slab, high_slab = joined[:EZ], joined[7 * EZ :]
            bottom = low_slab + jnp.where(
                row16 == 0, edge_image[2 * p : 2 * p + 1, :], roll(high_slab, 1, 0)
            )
            top = high_slab + jnp.where(
                row16 == EZ - 1, edge_image[2 * p + 1 : 2 * p + 2, :], roll(low_slab, -1, 0)
            )
            joined = jnp.concatenate([bottom, joined[EZ : 7 * EZ], top], axis=0)
            raw2 = operate(joined, shift)
            b_s[p] = right
            v_s[p] = joined
            right, joined = slabs_of(right), slabs_of(joined)
            mrow[p] = jnp.concatenate(
                [
                    total(product(right, right, 0.5) * inner_r),
                    total(product(right, raw, 1.0)),
                    total(product(joined, joined, 0.5) * inner_r),
                    total(product(joined, raw2, 1.0)),
                    jnp.zeros((4, 128), F32),
                ],
                axis=0,
            )

        sums = jnp.sum(
            jnp.concatenate([mrow[p] for p in range(4)], axis=0), axis=1, keepdims=True
        )
        row32, lane32 = sublanes((32, 128)), lanes((32, 128))
        mine = (row32 % 8 < 4) & (lane32 // 8 == (row32 // 8) * 4 + row32 % 8)
        moments = jnp.sum(jnp.where(mine, sums, 0.0), axis=0, keepdims=True)
        mom_s[...] = moments
        mom_r[z] = moments

        def send_moments(k, carry):
            pltpu.make_async_remote_copy(
                src_ref=mom_s,
                dst_ref=mom_r.at[z],
                send_sem=ms,
                recv_sem=mr_sem,
                device_id=(me, peer_z(k)),
                device_id_type=MESH,
            ).start()
            return carry

        lax.fori_loop(0, NZ - 1, send_moments, 0, unroll=True)
        view = mom_r.at[pl.ds(0, NZ - 1)]
        pltpu.make_async_copy(view, view, mr_sem).wait()
        pooled = mom_r[0]
        for at in range(1, NZ):
            pooled = pooled + mom_r[at]
        m0 = pooled
        m1, m2, m3 = (roll(pooled, -8 * k, 1) for k in range(1, 4))
        alpha0 = m0 / m1
        norm1 = alpha0 * alpha0 * m2 - m0
        gain = 1.0 + norm1 / m0
        curve = gain * gain * m1 - 2.0 * gain * alpha0 * m2 + alpha0 * alpha0 * m3
        alpha1 = norm1 / curve
        on_right = alpha0 + alpha1 * gain
        on_image = -alpha1 * alpha0
        lane1 = lanes((1, 128))
        for p in range(4):
            pick = lane1 == 32 * p
            first = jnp.sum(jnp.where(pick, on_right, 0.0), axis=1, keepdims=True)
            second = jnp.sum(jnp.where(pick, on_image, 0.0), axis=1, keepdims=True)
            factors[p] = jnp.concatenate(
                [first + jnp.zeros((1, 128), F32), second + jnp.zeros((1, 128), F32)]
                + [jnp.zeros((6, 128), F32)],
                axis=0,
            )

        pltpu.make_async_copy(view, view, ms).wait()
        await_tiles(recv1.at[0], NF - 1, s1.at[0])
        await_tiles(recv2, NF - 1, s2.at[0])

        @pl.when(owner1)
        def _():
            await_tiles(recv1.at[1], UNITS - FIRST - 1, s1.at[1])
            await_tiles(recv2, NF - 1, s2.at[1])

        @pl.when(jnp.logical_not(owner1))
        def _():
            await_tiles(recv1.at[1], UNITS - FIRST, s1.at[1])

    return kernel


def combine(right, image, factors, out, slots, sems):
    copies = []
    for p in range(4):
        mixed = factors[p, 0:1, 0:1] * right[p] + factors[p, 1:2, 0:1] * image[p]
        for h in range(2):
            for j in range(NODES):
                slots[p, h, pl.ds(j, EZ, stride=8), :] = mixed[
                    j * EZ : (j + 1) * EZ, 128 * h : 128 * h + 128
                ]
            copy = pltpu.make_async_copy(
                slots.at[p, h], out.at[p, :, pl.ds(128 * h, 128)], sems.at[2 * p + h]
            )
            copy.start()
            copies.append(copy)
    for copy in copies:
        copy.wait()


def solution(mesh):
    w256, w128, weights, derivative, stiffness = tables()
    kernel = make_kernel(weights, derivative, stiffness)

    def shards(vel_az, vel_rad, axial, metric_az, metric_rad):
        field = (4, ROWS, COLS)
        solved = pl.pallas_call(
            kernel,
            out_shape=(pltpu.VMEM(field, F32), pltpu.VMEM(field, F32), pltpu.VMEM((4, 8, 128), F32)),
            in_specs=[pl.BlockSpec(memory_space=pltpu.HBM)] * 7,
            out_specs=[pl.BlockSpec(memory_space=pltpu.VMEM)] * 3,
            scratch_shapes=[
                pltpu.VMEM((4, 2, ROWS, 128), F32),
                pltpu.VMEM((4, 2, ROWS, 128), F32),
                pltpu.VMEM((4, 2, ROWS, 128), F32),
                pltpu.VMEM((EZ, 32), F32),
                pltpu.VMEM((EZ, 32), F32),
                pltpu.VMEM(w256.shape, BF16),
                pltpu.VMEM(w128.shape, BF16),
                pltpu.VMEM((5, EZ, COLS), F32),
                pltpu.VMEM((ROWS, COLS), F32),
                pltpu.VMEM((4, ROWS, 128), F32),
                pltpu.VMEM((PADDED * 8, 128), F32),
                pltpu.VMEM((2, NF * 8, 128), F32),
                pltpu.VMEM((2, NF * 8, 128), F32),
                pltpu.VMEM((PADDED * 8, 128), F32),
                pltpu.VMEM((8, COLS), F32),
                pltpu.VMEM((2, 8, COLS), F32),
                pltpu.VMEM((16, COLS), F32),
                pltpu.VMEM((2, 16, COLS), F32),
                pltpu.VMEM((8, COLS), F32),
                pltpu.VMEM((8, COLS), F32),
                pltpu.VMEM((4, 8, 128), F32),
                pltpu.VMEM((1, 128), F32),
                pltpu.VMEM((NZ, 1, 128), F32),
                pltpu.SemaphoreType.DMA((29,)),
                pltpu.SemaphoreType.DMA((2,)),
                pltpu.SemaphoreType.DMA((2,)),
                pltpu.SemaphoreType.DMA((2,)),
                pltpu.SemaphoreType.DMA((2,)),
                pltpu.SemaphoreType.DMA((4,)),
                pltpu.SemaphoreType.DMA((4,)),
                pltpu.SemaphoreType.DMA(()),
                pltpu.SemaphoreType.DMA(()),
            ],
            compiler_params=pltpu.CompilerParams(
                collective_id=0, has_side_effects=True, vmem_limit_bytes=63488 * 1024
            ),
        )(
            vel_az,
            vel_rad,
            axial,
            metric_az,
            metric_rad,
            jnp.asarray(w256),
            jnp.asarray(w128),
        )
        return pl.pallas_call(
            combine,
            out_shape=jax.ShapeDtypeStruct(field, F32),
            in_specs=[pl.BlockSpec(memory_space=pltpu.VMEM)] * 3,
            out_specs=pl.BlockSpec(memory_space=pltpu.HBM),
            scratch_shapes=[pltpu.VMEM((4, 2, ROWS, 128), F32), pltpu.SemaphoreType.DMA((8,))],
            compiler_params=pltpu.CompilerParams(vmem_limit_bytes=16 * 2**20),
        )(*solved)

    spec = P("fourier", "elem", None)
    metric_spec = P("elem", None)
    return jax.shard_map(
        shards,
        mesh=mesh,
        in_specs=(spec, spec, spec, metric_spec, metric_spec),
        out_specs=spec,
        check_vma=False,
    )
```

```python
import math

import jax
import jax.numpy as jnp
import ml_dtypes
import numpy as np
from jax import lax
from jax.experimental import pallas as pl
from jax.experimental.pallas import tpu as pltpu
from jax.sharding import PartitionSpec as P

MESH = pl.DeviceIdType.MESH
F32 = jnp.float32
BF16 = jnp.bfloat16
HIGH = lax.Precision.HIGHEST

PLANES = 256
NODES = 8
NF = 64
NZ = 16
ROWS = 128
COLS = 256
EZ = 16
UNIQUE = 7 * EZ
A_UNITS = 56
X_UNIT = 56
B_BASE = 57
UNITS = 99
PADDED = 105
FIRST = 64
EXTRA = (1, 27, 45)

DR_H, DR_L, SR, KR_H, KR_L, ER, C_H, C_L = range(8)
RA_B, EA_B = range(2)


def gll_tables():
    points = np.array(
        [
            -1.0,
            -0.8717401485096066,
            -0.5917001814331423,
            -0.2092992179024789,
            0.2092992179024789,
            0.5917001814331423,
            0.8717401485096066,
            1.0,
        ]
    )
    gll_weights = np.array(
        [
            0.03571428571428571,
            0.2107042271435061,
            0.3411226924835044,
            0.4124587946587038,
            0.4124587946587038,
            0.3411226924835044,
            0.2107042271435061,
            0.03571428571428571,
        ]
    )
    number = points.shape[0]
    scales = np.array(
        [
            np.prod([points[col_at] - points[other] for other in range(number) if other != col_at])
            for col_at in range(number)
        ]
    )
    derivative = np.zeros((number, number))
    for row_at in range(number):
        for col_at in range(number):
            if row_at != col_at:
                derivative[row_at, col_at] = scales[row_at] / (
                    scales[col_at] * (points[row_at] - points[col_at])
                )
    for row_at in range(number):
        derivative[row_at, row_at] = -np.sum(derivative[row_at])
    stiffness = derivative.T @ (gll_weights[:, None] * derivative)
    return (
        gll_weights.astype(np.float32),
        derivative.astype(np.float32),
        stiffness.astype(np.float32),
    )


def mode_table():
    modes = np.arange(PLANES)
    waves = np.where(modes == 1, PLANES // 2, modes // 2)
    phase = waves[:, None] * np.arange(PLANES)[None, :] % PLANES
    angles = phase * (2.0 * math.pi / PLANES)
    odd = (modes % 2 == 1) & (modes > 1)
    return (np.where(odd[:, None], -np.sin(angles), np.cos(angles)) / math.sqrt(PLANES)).astype(
        np.float32
    )


def halves(matrix):
    high = matrix.astype(ml_dtypes.bfloat16)
    low = (matrix - high.astype(np.float32)).astype(ml_dtypes.bfloat16)
    return [high, low]


def row_map():
    every = [(e, j) for e in range(EZ) for j in range(7)]
    second = {}
    for g in range(2):
        for q in range(4):
            j = g * 4 + q
            second[q * 16 + g] = (0, j) if j < 7 else (1, 0)
            if j < 7:
                second[(4 + q) * 16 + g] = (EZ - 1, j)
    left = [r for r in every if r not in second.values()]
    for block in range(8):
        for g in range(14):
            if block * 16 + g not in second:
                second[block * 16 + g] = left.pop(0)
    return second


def tables():
    weights, derivative, stiffness = gll_tables()
    w256 = halves(np.kron(np.eye(32, dtype=np.float32), derivative).T)
    fold = np.zeros((COLS, COLS), np.float32)
    for s in range(COLS):
        c = 7 * (s // 8) + s % 8
        if c < 224:
            fold[s, c] = 1.0
    w256 += [fold.astype(ml_dtypes.bfloat16)]
    w256 += halves(np.kron(np.eye(32, dtype=np.float32), stiffness).T)
    w256 += [fold.T.astype(ml_dtypes.bfloat16)]
    w256 += halves(mode_table())
    fold_rows = np.zeros((ROWS, ROWS), np.float32)
    for at, (e, j) in row_map().items():
        fold_rows[at, j * EZ + e] = 1.0
        if j == 0 and e > 0:
            fold_rows[at, 7 * EZ + e - 1] = 1.0
    unfold_rows = fold_rows.T.copy()
    unfold_rows[ROWS - 1, 14] = 1.0
    w128 = [m.astype(ml_dtypes.bfloat16) for m in (fold_rows, unfold_rows)]
    return np.stack(w256), np.stack(w128), weights, derivative, stiffness


def split(x):
    high = x.astype(BF16)
    return high, (x - high.astype(F32)).astype(BF16)


def dot(a, b):
    return jnp.dot(a, b, preferred_element_type=F32)


def left3(high, low, x):
    xh, xl = split(x)
    return dot(high, xh) + dot(high, xl) + dot(low, xh)


def right3(x, high, low):
    xh, xl = split(x)
    return dot(xh, high) + dot(xl, high) + dot(xh, low)


def right2(x, matrix):
    xh, xl = split(x)
    return dot(xh, matrix) + dot(xl, matrix)


def roll(x, shift, axis):
    size = x.shape[axis]
    shift %= size
    return pltpu.roll(x, shift, axis) if shift else x


def lanes(shape):
    return lax.broadcasted_iota(jnp.int32, shape, 1)


def sublanes(shape):
    return lax.broadcasted_iota(jnp.int32, shape, 0)


def join_cols(field):
    lane = lanes(field.shape)
    total = (
        field
        + jnp.where((lane % 8 == 7), roll(field, -1, 1), 0.0)
        + jnp.where((lane % 8 == 0) & (lane > 0), roll(field, 1, 1), 0.0)
    )
    return jnp.where(lane == COLS - 1, 0.0, total)


def along(matrix, slabs, j):
    total = float(matrix[j, 0]) * slabs[0]
    for i in range(1, NODES):
        total = total + float(matrix[j, i]) * slabs[i]
    return total


def make_kernel(weights, derivative, stiffness):
    def kernel(
        va_hbm,
        vr_hbm,
        ax_hbm,
        ma_hbm,
        mr_hbm,
        w256_hbm,
        w128_hbm,
        b_s,
        v_s,
        factors,
        va,
        vr,
        ax,
        ma_s,
        mr_s,
        w256,
        w128,
        metric,
        x_s,
        r_s,
        packed_b,
        send1,
        recv1,
        send2,
        recv2,
        meet_s,
        meet_r,
        edge_s,
        edge_r,
        edge_image,
        edge_right,
        mrow,
        mom_s,
        mom_r,
        in_sem,
        s1,
        r1,
        s2,
        r2,
        hs,
        hr,
        ms,
        mr_sem,
        known,
    ):
        me = lax.axis_index("fourier")
        z = lax.axis_index("elem")
        up, down = lax.rem(z + 1, NZ), lax.rem(z + NZ - 1, NZ)

        barrier = pltpu.get_barrier_semaphore()

        def far_first(k, size):
            step = (k + 1) // 2
            return size // 2 + step * (1 - 2 * lax.rem(k, 2))

        def peer_f(k):
            row, col, core = me // 8, lax.rem(me // 2, 4), lax.rem(me, 2)
            row = lax.rem(row + far_first(k // 8, 8), 8)
            col = lax.rem(col + far_first(lax.rem(k // 2, 4), 4), 4)
            core = lax.rem(core + 1 + lax.rem(k, 2), 2)
            return row * 8 + col * 2 + core

        def peer_z(k):
            return lax.rem(z + far_first(k, NZ), NZ)

        def greet_f(k, carry):
            pl.semaphore_signal(barrier, inc=1, device_id=(peer_f(k), z), device_id_type=MESH)
            return carry

        for target in (up, down):
            pl.semaphore_signal(barrier, inc=1, device_id=(me, target), device_id_type=MESH)
        lax.fori_loop(0, NF - 1, greet_f, 0, unroll=True)

        loads = [
            pltpu.make_async_copy(src, dst, in_sem.at[i])
            for i, (src, dst) in enumerate(
                [(ma_hbm, ma_s), (mr_hbm, mr_s)]
                + [(ref.at[p, :, pl.ds(128 * h, 128)], to.at[p, h]) for p in range(4) for ref, to in ((ax_hbm, ax), (va_hbm, va), (vr_hbm, vr)) for h in range(2)]
                + [(w256_hbm.at[pl.ds(0, KR_H)], w256.at[pl.ds(0, KR_H)]), (w128_hbm, w128)]
            )
        ]
        late = pltpu.make_async_copy(
            w256_hbm.at[pl.ds(KR_H, 8 - KR_H)], w256.at[pl.ds(KR_H, 8 - KR_H)], in_sem.at[28]
        )
        for load in loads:
            load.start()
        recv2[pl.ds(UNITS * 8, (PADDED - UNITS) * 8), :] = jnp.zeros(
            ((PADDED - UNITS) * 8, 128), F32
        )

        for load in loads[:2]:
            load.wait()
        up_cols = (sublanes((32, COLS)) == lanes((32, COLS)) // 8).astype(F32)
        wide = jnp.dot(
            jnp.concatenate([ma_s[...], mr_s[...]], axis=0),
            up_cols,
            precision=HIGH,
            preferred_element_type=F32,
        )
        metric_a, metric_r = wide[:EZ], wide[EZ:]

        def end_weights(shape):
            place = lanes(shape) % 8
            place = jnp.minimum(place, 7 - place)
            value = jnp.full(shape, float(weights[3]), F32)
            for at in range(3):
                value = jnp.where(place == at, float(weights[at]), value)
            return value

        weight_r = end_weights((1, COLS))
        metric[0] = metric_a
        metric[1] = metric_r
        metric[2] = weight_r / (metric_a * metric_r)
        metric[3] = metric_a / metric_r * weight_r
        metric[4] = metric_r / metric_a
        meet_s[...] = jnp.zeros((8, COLS), F32)
        for row, values in enumerate((metric_a, metric_r)):
            meet_s[2 * row : 2 * row + 1, :] = values[0:1]
            meet_s[2 * row + 1 : 2 * row + 2, :] = values[EZ - 1 :]

        for load in loads[26:]:
            load.wait()

        lane128 = lanes((16, 128))

        row16 = sublanes((EZ, COLS))
        for p in range(4):
            for load in loads[2 + 6 * p : 8 + 6 * p]:
                load.wait()

            def slab_of(ref, j, p=p):
                return jnp.concatenate(
                    [ref[p, h, pl.ds(j, EZ, stride=8), :] for h in range(2)], axis=1
                )

            slabs = [slab_of(ax, j) for j in range(NODES)]
            for j in range(NODES):
                x_s[j * EZ : (j + 1) * EZ, :] = slabs[j]
            x_all = x_s[0:ROWS, :]
            grad_r = right3(x_all, w256[DR_H], w256[DR_L])
            loaded = []
            for j in range(NODES):
                grad_a = along(derivative, slabs, j)
                nonlinear = slab_of(va, j) * (grad_a * metric[0]) + slab_of(vr, j) * (
                    grad_r[j * EZ : (j + 1) * EZ] * metric[1]
                )
                loaded.append(
                    (2.0 * slabs[j] - nonlinear) * ((2.0 * float(weights[j])) * metric[2])
                )
            folded = right2(jnp.concatenate(loaded, axis=0), w256[SR])
            last = folded[ROWS - 1 :]
            for h in range(2):
                send1[X_UNIT * 8 + 2 * p + h : X_UNIT * 8 + 2 * p + h + 1, :] = last[
                    :, 128 * h : 128 * h + 128
                ]
            start = folded[:EZ, :128] + jnp.where(
                row16[:, :128] > 0, roll(folded[7 * EZ :, :128], 1, 0), 0.0
            )
            for j in range(7):
                slab = start if j == 0 else folded[j * EZ : (j + 1) * EZ, :128]
                for h in range(2):
                    send1[pl.ds(64 * j + 2 * p + h, 8, stride=8), :] = slab[8 * h : 8 * h + 8]
            high, low = split(folded[:, 128:])
            packed = dot(w128[RA_B], high) + dot(w128[RA_B], low)
            for h in range(2):
                quarters = [packed[(4 * h + q) * 16 : (4 * h + q + 1) * 16] for q in range(4)]
                for t in range(3):
                    tile = roll(quarters[0], -32 * t, 1)
                    for q in range(1, 4):
                        tile = jnp.where(lane128 >= 32 * q, roll(quarters[q], 32 * (q - t), 1), tile)
                    send1[pl.ds((B_BASE + t) * 8 + 2 * p + h, 16, stride=24), :] = tile
        late.start()

        pl.semaphore_wait(barrier, NF - 1 + 2)

        def exchange(src, dst, at):
            copies = [
                pltpu.make_async_remote_copy(
                    src_ref=src,
                    dst_ref=dst.at[side],
                    send_sem=hs.at[at + side],
                    recv_sem=hr.at[at + side],
                    device_id=(me, target),
                    device_id_type=MESH,
                )
                for side, target in ((0, up), (1, down))
            ]
            for copy in copies:
                copy.start()
            return copies

        def spread_entry(at, reach):
            for step in (reach, NZ - reach):
                pl.semaphore_signal(
                    known.at[at],
                    inc=1,
                    device_id=(me, lax.rem(z + step, NZ)),
                    device_id_type=MESH,
                )
            pl.semaphore_wait(known.at[at], 2)

        def tile_at(index):
            return pl.ds(pl.multiple_of(index * 8, 8), 8)

        def send_plane(unit, slot, target):
            pltpu.make_async_remote_copy(
                src_ref=send1.at[tile_at(unit), :],
                dst_ref=recv1.at[slot, tile_at(me), :],
                send_sem=s1.at[slot],
                recv_sem=r1.at[slot],
                device_id=(target, z),
                device_id_type=MESH,
            ).start()

        def first_chunk(k, carry):
            target = peer_f(k)
            send_plane(target, 0, target)
            return carry

        def second_chunk(k, carry):
            row = lax.rem(me // 8 + far_first(k // 4, 8), 8)
            col = lax.rem(me // 2 + far_first(lax.rem(k, 4), 4), 4)
            chip = row * 4 + col

            @pl.when(2 * chip != me)
            def _():
                send_plane(FIRST + chip, 1, 2 * chip)

            return carry

        for at, target in enumerate(EXTRA):

            @pl.when(me != target)
            def _(at=at, target=target):
                send_plane(FIRST + NF // 2 + at, 1, target)

        lax.fori_loop(0, NF - 1, first_chunk, 0, unroll=True)
        meets = exchange(meet_s, meet_r, 0)
        lax.fori_loop(0, NF // 2, second_chunk, 0, unroll=True)
        spread_entry(0, 1)
        unit1 = FIRST + me // 2
        owner1 = me % 2 == 0
        for at, target in enumerate(EXTRA):
            unit1 = jnp.where(me == target, FIRST + NF // 2 + at, unit1)
            owner1 = owner1 | (me == target)

        recv1[0, tile_at(me), :] = send1[tile_at(me), :]

        def await_tiles(ref, count, sem):
            view = ref.at[pl.ds(0, count * 8), :]
            pltpu.make_async_copy(view, view, sem).wait()

        def transform(slot, unit):
            x = jnp.concatenate(
                [recv1[slot, pl.ds(h, PLANES, stride=2), :] for h in range(2)], axis=1
            )
            y = left3(w256[C_H], w256[C_L], x)
            for h in range(2):
                send2[slot, pl.ds(h, PLANES, stride=2), :] = y[:, 128 * h : 128 * (h + 1)]

            def send_modes(k, carry):
                target = peer_f(k)
                pltpu.make_async_remote_copy(
                    src_ref=send2.at[slot, tile_at(target), :],
                    dst_ref=recv2.at[tile_at(unit), :],
                    send_sem=s2.at[slot],
                    recv_sem=r2.at[slot],
                    device_id=(target, z),
                    device_id_type=MESH,
                ).start()
                return carry

            lax.fori_loop(0, NF - 1, send_modes, 0, unroll=True)
            recv2[tile_at(unit), :] = send2[slot, tile_at(me), :]

        late.wait()
        await_tiles(recv1.at[0], NF - 1, r1.at[0])
        transform(0, me)
        spread_entry(1, 2)

        @pl.when(owner1)
        def _():
            recv1[1, tile_at(me), :] = send1[tile_at(unit1), :]
            await_tiles(recv1.at[1], NF - 1, r1.at[1])
            transform(1, unit1)

        spread_entry(2, 4)

        await_tiles(recv2, NF - 1, r2.at[0])
        even = sublanes((8, 128)) % 2 == 0
        lane = lanes((8, 128))
        sub = sublanes((8, COLS))
        low_side = sub % 2 == 0
        x_tile = recv2[X_UNIT * 8 : X_UNIT * 8 + 8, :]
        edge_rows = []
        for j in range(8):
            g, q = j // 4, j % 4
            start, end = (8 * j, 8 * j + 7) if j < 7 else (1, X_UNIT)
            part_a = jnp.where(
                even,
                recv2[8 * start : 8 * start + 8, :],
                recv2[8 * end : 8 * end + 8, :] if j < 7 else roll(x_tile, 1, 0),
            )
            pieces = [
                recv2[(B_BASE + 3 * g + t) * 8 : (B_BASE + 3 * g + t) * 8 + 8, :] for t in range(3)
            ]
            part_b = roll(pieces[0], -32 * q, 1)
            for t in range(1, 3):
                part_b = jnp.where(lane >= 32 * t, roll(pieces[t], 32 * (t - q), 1), part_b)
            if j == 7:
                part_b = jnp.where(even, part_b, x_tile)
            edge_rows.append(jnp.concatenate([part_a, part_b], axis=1))
        edge = right2(jnp.concatenate(edge_rows, axis=0), w256[ER])
        along_a = jnp.zeros((8, COLS), F32)
        for j in range(8):
            factor = jnp.where(low_side, float(stiffness[0, j]), float(stiffness[7, j]))
            along_a = along_a + factor * edge[8 * j : 8 * j + 8]
        chosen = jnp.where(low_side, edge[0:8], edge[56:64])
        along_r = right3(chosen, w256[KR_H], w256[KR_L])

        def edge_coef(at):
            return jnp.where(low_side, metric[at, 0:1, :], metric[at, EZ - 1 : EZ, :])

        def shift_of(mode):
            wave = jnp.where(mode == 1, PLANES // 2, mode // 2)
            return 4.0 + (wave.astype(F32) * 0.03125) * (wave.astype(F32) * 0.03125)

        edge_shift = shift_of(4 * me + sub // 2)
        end = float(weights[0])
        image = (
            edge_coef(3) * along_a
            + (end * edge_coef(4)) * along_r
            + edge_shift * (end * edge_coef(2)) * chosen
        )
        edge_s[0:8, :] = join_cols(image)
        edge_s[8:16, :] = chosen
        edges = exchange(edge_s, edge_r, 2)

        for copy in meets:
            copy.wait()
        next_a = jnp.where(low_side, meet_r[0, 1:2, :], meet_r[1, 0:1, :])
        next_r = jnp.where(low_side, meet_r[0, 3:4, :], meet_r[1, 2:3, :])
        corner = jnp.where(low_side, float(stiffness[7, 7]), float(stiffness[0, 0]))
        across = join_cols(
            next_a / next_r * weight_r * (corner * chosen)
            + (end * (next_r / next_a)) * along_r
            + edge_shift * (end * (weight_r / (next_a * next_r))) * chosen
        )

        for copy in edges:
            copy.wait()
        below, above = edge_r[0], edge_r[1]
        edge_image[...] = across + jnp.where(
            low_side, roll(below[0:8], -1, 0), roll(above[0:8], 1, 0)
        )
        edge_right[...] = jnp.where(low_side, roll(below[8:16], -1, 0), roll(above[8:16], 1, 0))

        @pl.when(owner1)
        def _():
            await_tiles(recv2, UNITS - FIRST - 1, r2.at[1])

        @pl.when(jnp.logical_not(owner1))
        def _():
            await_tiles(recv2, UNITS - FIRST, r2.at[1])

        for p in range(4):
            for h in range(2):
                pieces = [
                    recv2[pl.ds((B_BASE + t) * 8 + 2 * p + h, 16, stride=24), :] for t in range(3)
                ]
                for q in range(4):
                    part_b = roll(pieces[0], -32 * q, 1)
                    for t in range(1, 3):
                        part_b = jnp.where(
                            lane128 >= 32 * t, roll(pieces[t], 32 * (t - q), 1), part_b
                        )
                    if h == 0 and q == 0:
                        part_b = jnp.where(
                            sublanes((16, 128)) == 14, x_tile[2 * p + 1 : 2 * p + 2, :], part_b
                        )
                    packed_b[p, (4 * h + q) * 16 : (4 * h + q + 1) * 16, :] = part_b

        lane_r = lanes((1, COLS))
        inner_r = jnp.where(
            ((lane_r % 8 == 7) & (lane_r < COLS - 1)) | ((lane_r % 8 == 0) & (lane_r > 0)), 0.5, 1.0
        )

        def slabs_of(field):
            return [field[j * EZ : (j + 1) * EZ] for j in range(NODES)]

        def operate(slabs, along_r, shift):
            heavy = shift * metric[2]
            return [
                metric[3] * along(stiffness, slabs, j)
                + float(weights[j]) * (metric[4] * along_r[j] + heavy * slabs[j])
                for j in range(NODES)
            ]

        def product(left, right, ends):
            total = ends * (left[0] * right[0] + left[7] * right[7])
            for j in range(1, 7):
                total = total + left[j] * right[j]
            return total

        def total(field):
            row = jnp.sum(field, axis=0, keepdims=True)
            return row[:, :128] + row[:, 128:]

        for p in range(4):
            left_cols = []
            for j in range(7):
                left_cols += [recv2[pl.ds(64 * j + 2 * p + h, 8, stride=8), :] for h in range(2)]
            first_slab = jnp.concatenate(left_cols[:2], axis=0)
            left_cols.append(
                jnp.where(
                    row16[:, :128] == EZ - 1, x_tile[2 * p : 2 * p + 1, :], roll(first_slab, -1, 0)
                )
            )
            high, low = split(packed_b[p])
            right_cols = dot(w128[EA_B], high) + dot(w128[EA_B], low)
            x_s[ROWS * p : ROWS * (p + 1), :] = jnp.concatenate(
                [jnp.concatenate(left_cols, axis=0), right_cols], axis=1
            )
        x_s[...] = right2(x_s[...], w256[ER])
        for p in range(4):
            top = ROWS * p
            x_s[top : top + 8, :] = x_s[top : top + 8, :] + jnp.where(
                sub == 0, edge_right[2 * p : 2 * p + 1, :], 0.0
            )
            top = ROWS * (p + 1) - 8
            x_s[top : top + 8, :] = x_s[top : top + 8, :] + jnp.where(
                sub == 7, edge_right[2 * p + 1 : 2 * p + 2, :], 0.0
            )
        r_s[...] = right3(x_s[...], w256[KR_H], w256[KR_L])
        for p in range(4):
            at = ROWS * p
            b_s[p] = x_s[at : at + ROWS, :]
            right = slabs_of(b_s[p])
            raw = operate(right, slabs_of(r_s[at : at + ROWS, :]), shift_of(4 * me + p))
            joined = join_cols(jnp.concatenate(raw, axis=0))
            low_slab, high_slab = joined[:EZ], joined[7 * EZ :]
            bottom = low_slab + jnp.where(
                row16 == 0, edge_image[2 * p : 2 * p + 1, :], roll(high_slab, 1, 0)
            )
            top = high_slab + jnp.where(
                row16 == EZ - 1, edge_image[2 * p + 1 : 2 * p + 2, :], roll(low_slab, -1, 0)
            )
            joined = jnp.concatenate([bottom, joined[EZ : 7 * EZ], top], axis=0)
            v_s[p] = joined
            joined = slabs_of(joined)
            mrow[p, 0:1, :] = total(product(right, right, 0.5) * inner_r)
            mrow[p, 1:2, :] = total(product(right, raw, 1.0))
            mrow[p, 2:3, :] = total(product(joined, joined, 0.5) * inner_r)
            mrow[p, 4:8, :] = jnp.zeros((4, 128), F32)
        for p in range(4):
            x_s[ROWS * p : ROWS * (p + 1), :] = v_s[p]
        r_s[...] = right3(x_s[...], w256[KR_H], w256[KR_L])
        for p in range(4):
            at = ROWS * p
            joined = slabs_of(v_s[p])
            raw = operate(joined, slabs_of(r_s[at : at + ROWS, :]), shift_of(4 * me + p))
            mrow[p, 3:4, :] = total(product(joined, raw, 1.0))

        sums = jnp.sum(
            jnp.concatenate([mrow[p] for p in range(4)], axis=0), axis=1, keepdims=True
        )
        row32, lane32 = sublanes((32, 128)), lanes((32, 128))
        mine = (row32 % 8 < 4) & (lane32 // 8 == (row32 // 8) * 4 + row32 % 8)
        moments = jnp.sum(jnp.where(mine, sums, 0.0), axis=0, keepdims=True)
        mom_s[...] = moments
        mom_r[z] = moments

        def send_moments(k, carry):
            pltpu.make_async_remote_copy(
                src_ref=mom_s,
                dst_ref=mom_r.at[z],
                send_sem=ms,
                recv_sem=mr_sem,
                device_id=(me, peer_z(k)),
                device_id_type=MESH,
            ).start()
            return carry

        lax.fori_loop(0, NZ - 1, send_moments, 0, unroll=True)
        view = mom_r.at[pl.ds(0, NZ - 1)]
        pltpu.make_async_copy(view, view, mr_sem).wait()
        pooled = mom_r[0]
        for at in range(1, NZ):
            pooled = pooled + mom_r[at]
        m0 = pooled
        m1, m2, m3 = (roll(pooled, -8 * k, 1) for k in range(1, 4))
        alpha0 = m0 / m1
        norm1 = alpha0 * alpha0 * m2 - m0
        gain = 1.0 + norm1 / m0
        curve = gain * gain * m1 - 2.0 * gain * alpha0 * m2 + alpha0 * alpha0 * m3
        alpha1 = norm1 / curve
        on_right = alpha0 + alpha1 * gain
        on_image = -alpha1 * alpha0
        lane1 = lanes((1, 128))
        for p in range(4):
            pick = lane1 == 32 * p
            first = jnp.sum(jnp.where(pick, on_right, 0.0), axis=1, keepdims=True)
            second = jnp.sum(jnp.where(pick, on_image, 0.0), axis=1, keepdims=True)
            factors[p] = jnp.concatenate(
                [first + jnp.zeros((1, 128), F32), second + jnp.zeros((1, 128), F32)]
                + [jnp.zeros((6, 128), F32)],
                axis=0,
            )

        pltpu.make_async_copy(view, view, ms).wait()
        await_tiles(recv1.at[0], NF - 1, s1.at[0])
        await_tiles(recv2, NF - 1, s2.at[0])

        @pl.when(owner1)
        def _():
            await_tiles(recv1.at[1], UNITS - FIRST - 1, s1.at[1])
            await_tiles(recv2, NF - 1, s2.at[1])

        @pl.when(jnp.logical_not(owner1))
        def _():
            await_tiles(recv1.at[1], UNITS - FIRST, s1.at[1])

    return kernel


def combine(right, image, factors, out, slots, sems):
    copies = []
    for p in range(4):
        mixed = factors[p, 0:1, 0:1] * right[p] + factors[p, 1:2, 0:1] * image[p]
        for h in range(2):
            for j in range(NODES):
                slots[p, h, pl.ds(j, EZ, stride=8), :] = mixed[
                    j * EZ : (j + 1) * EZ, 128 * h : 128 * h + 128
                ]
            copy = pltpu.make_async_copy(
                slots.at[p, h], out.at[p, :, pl.ds(128 * h, 128)], sems.at[2 * p + h]
            )
            copy.start()
            copies.append(copy)
    for copy in copies:
        copy.wait()


def solution(mesh):
    w256, w128, weights, derivative, stiffness = tables()
    kernel = make_kernel(weights, derivative, stiffness)

    def shards(vel_az, vel_rad, axial, metric_az, metric_rad):
        field = (4, ROWS, COLS)
        solved = pl.pallas_call(
            kernel,
            out_shape=(pltpu.VMEM(field, F32), pltpu.VMEM(field, F32), pltpu.VMEM((4, 8, 128), F32)),
            in_specs=[pl.BlockSpec(memory_space=pltpu.HBM)] * 7,
            out_specs=[pl.BlockSpec(memory_space=pltpu.VMEM)] * 3,
            scratch_shapes=[
                pltpu.VMEM((4, 2, ROWS, 128), F32),
                pltpu.VMEM((4, 2, ROWS, 128), F32),
                pltpu.VMEM((4, 2, ROWS, 128), F32),
                pltpu.VMEM((EZ, 32), F32),
                pltpu.VMEM((EZ, 32), F32),
                pltpu.VMEM(w256.shape, BF16),
                pltpu.VMEM(w128.shape, BF16),
                pltpu.VMEM((5, EZ, COLS), F32),
                pltpu.VMEM((4 * ROWS, COLS), F32),
                pltpu.VMEM((4 * ROWS, COLS), F32),
                pltpu.VMEM((4, ROWS, 128), F32),
                pltpu.VMEM((PADDED * 8, 128), F32),
                pltpu.VMEM((2, NF * 8, 128), F32),
                pltpu.VMEM((2, NF * 8, 128), F32),
                pltpu.VMEM((PADDED * 8, 128), F32),
                pltpu.VMEM((8, COLS), F32),
                pltpu.VMEM((2, 8, COLS), F32),
                pltpu.VMEM((16, COLS), F32),
                pltpu.VMEM((2, 16, COLS), F32),
                pltpu.VMEM((8, COLS), F32),
                pltpu.VMEM((8, COLS), F32),
                pltpu.VMEM((4, 8, 128), F32),
                pltpu.VMEM((1, 128), F32),
                pltpu.VMEM((NZ, 1, 128), F32),
                pltpu.SemaphoreType.DMA((29,)),
                pltpu.SemaphoreType.DMA((2,)),
                pltpu.SemaphoreType.DMA((2,)),
                pltpu.SemaphoreType.DMA((2,)),
                pltpu.SemaphoreType.DMA((2,)),
                pltpu.SemaphoreType.DMA((4,)),
                pltpu.SemaphoreType.DMA((4,)),
                pltpu.SemaphoreType.DMA(()),
                pltpu.SemaphoreType.DMA(()),
                pltpu.SemaphoreType.REGULAR((3,)),
            ],
            compiler_params=pltpu.CompilerParams(
                collective_id=0, has_side_effects=True, vmem_limit_bytes=63488 * 1024
            ),
        )(
            vel_az,
            vel_rad,
            axial,
            metric_az,
            metric_rad,
            jnp.asarray(w256),
            jnp.asarray(w128),
        )
        return pl.pallas_call(
            combine,
            out_shape=jax.ShapeDtypeStruct(field, F32),
            in_specs=[pl.BlockSpec(memory_space=pltpu.VMEM)] * 3,
            out_specs=pl.BlockSpec(memory_space=pltpu.HBM),
            scratch_shapes=[pltpu.VMEM((4, 2, ROWS, 128), F32), pltpu.SemaphoreType.DMA((8,))],
            compiler_params=pltpu.CompilerParams(vmem_limit_bytes=16 * 2**20),
        )(*solved)

    spec = P("fourier", "elem", None)
    metric_spec = P("elem", None)
    return jax.shard_map(
        shards,
        mesh=mesh,
        in_specs=(spec, spec, spec, metric_spec, metric_spec),
        out_specs=spec,
        check_vma=False,
    )
```

```python
import math

import jax
import jax.numpy as jnp
import ml_dtypes
import numpy as np
from jax import lax
from jax.experimental import pallas as pl
from jax.experimental.pallas import tpu as pltpu
from jax.sharding import PartitionSpec as P

MESH = pl.DeviceIdType.MESH
F32 = jnp.float32
BF16 = jnp.bfloat16
HIGH = lax.Precision.HIGHEST

PLANES = 256
NODES = 8
NF = 64
NZ = 16
ROWS = 128
COLS = 256
EZ = 16
UNIQUE = 7 * EZ
A_UNITS = 56
X_UNIT = 56
B_BASE = 57
UNITS = 99
PADDED = 105
FIRST = 64
EXTRA = (1, 27, 45)

DR_H, DR_L, SR, KR_H, KR_L, ER, C_H, C_L = range(8)
RA_B, EA_B = range(2)


def gll_tables():
    points = np.array(
        [
            -1.0,
            -0.8717401485096066,
            -0.5917001814331423,
            -0.2092992179024789,
            0.2092992179024789,
            0.5917001814331423,
            0.8717401485096066,
            1.0,
        ]
    )
    gll_weights = np.array(
        [
            0.03571428571428571,
            0.2107042271435061,
            0.3411226924835044,
            0.4124587946587038,
            0.4124587946587038,
            0.3411226924835044,
            0.2107042271435061,
            0.03571428571428571,
        ]
    )
    number = points.shape[0]
    scales = np.array(
        [
            np.prod([points[col_at] - points[other] for other in range(number) if other != col_at])
            for col_at in range(number)
        ]
    )
    derivative = np.zeros((number, number))
    for row_at in range(number):
        for col_at in range(number):
            if row_at != col_at:
                derivative[row_at, col_at] = scales[row_at] / (
                    scales[col_at] * (points[row_at] - points[col_at])
                )
    for row_at in range(number):
        derivative[row_at, row_at] = -np.sum(derivative[row_at])
    stiffness = derivative.T @ (gll_weights[:, None] * derivative)
    return (
        gll_weights.astype(np.float32),
        derivative.astype(np.float32),
        stiffness.astype(np.float32),
    )


def mode_table():
    modes = np.arange(PLANES)
    waves = np.where(modes == 1, PLANES // 2, modes // 2)
    phase = waves[:, None] * np.arange(PLANES)[None, :] % PLANES
    angles = phase * (2.0 * math.pi / PLANES)
    odd = (modes % 2 == 1) & (modes > 1)
    return (np.where(odd[:, None], -np.sin(angles), np.cos(angles)) / math.sqrt(PLANES)).astype(
        np.float32
    )


def halves(matrix):
    high = matrix.astype(ml_dtypes.bfloat16)
    low = (matrix - high.astype(np.float32)).astype(ml_dtypes.bfloat16)
    return [high, low]


def row_map():
    every = [(e, j) for e in range(EZ) for j in range(7)]
    second = {}
    for g in range(2):
        for q in range(4):
            j = g * 4 + q
            second[q * 16 + g] = (0, j) if j < 7 else (1, 0)
            if j < 7:
                second[(4 + q) * 16 + g] = (EZ - 1, j)
    left = [r for r in every if r not in second.values()]
    for block in range(8):
        for g in range(14):
            if block * 16 + g not in second:
                second[block * 16 + g] = left.pop(0)
    return second


def tables():
    weights, derivative, stiffness = gll_tables()
    w256 = halves(np.kron(np.eye(32, dtype=np.float32), derivative).T)
    fold = np.zeros((COLS, COLS), np.float32)
    for s in range(COLS):
        c = 7 * (s // 8) + s % 8
        if c < 224:
            fold[s, c] = 1.0
    w256 += [fold.astype(ml_dtypes.bfloat16)]
    w256 += halves(np.kron(np.eye(32, dtype=np.float32), stiffness).T)
    w256 += [fold.T.astype(ml_dtypes.bfloat16)]
    w256 += halves(mode_table())
    fold_rows = np.zeros((ROWS, ROWS), np.float32)
    for at, (e, j) in row_map().items():
        fold_rows[at, j * EZ + e] = 1.0
        if j == 0 and e > 0:
            fold_rows[at, 7 * EZ + e - 1] = 1.0
    unfold_rows = fold_rows.T.copy()
    unfold_rows[ROWS - 1, 14] = 1.0
    w128 = [m.astype(ml_dtypes.bfloat16) for m in (fold_rows, unfold_rows)]
    return np.stack(w256), np.stack(w128), weights, derivative, stiffness


def split(x):
    high = x.astype(BF16)
    return high, (x - high.astype(F32)).astype(BF16)


def dot(a, b):
    return jnp.dot(a, b, preferred_element_type=F32)


def left3(high, low, x):
    xh, xl = split(x)
    return dot(high, xh) + dot(high, xl) + dot(low, xh)


def right3(x, high, low):
    xh, xl = split(x)
    return dot(xh, high) + dot(xl, high) + dot(xh, low)


def right2(x, matrix):
    xh, xl = split(x)
    return dot(xh, matrix) + dot(xl, matrix)


def roll(x, shift, axis):
    size = x.shape[axis]
    shift %= size
    return pltpu.roll(x, shift, axis) if shift else x


def lanes(shape):
    return lax.broadcasted_iota(jnp.int32, shape, 1)


def sublanes(shape):
    return lax.broadcasted_iota(jnp.int32, shape, 0)


def join_cols(field):
    lane = lanes(field.shape)
    total = (
        field
        + jnp.where((lane % 8 == 7), roll(field, -1, 1), 0.0)
        + jnp.where((lane % 8 == 0) & (lane > 0), roll(field, 1, 1), 0.0)
    )
    return jnp.where(lane == COLS - 1, 0.0, total)


def along(matrix, slabs, j):
    total = float(matrix[j, 0]) * slabs[0]
    for i in range(1, NODES):
        total = total + float(matrix[j, i]) * slabs[i]
    return total


def make_kernel(weights, derivative, stiffness):
    def kernel(
        va_hbm,
        vr_hbm,
        ax_hbm,
        ma_hbm,
        mr_hbm,
        w256_hbm,
        w128_hbm,
        b_s,
        v_s,
        factors,
        va,
        vr,
        ax,
        ma_s,
        mr_s,
        w256,
        w128,
        metric,
        x_s,
        r_s,
        packed_b,
        send1,
        recv1,
        send2,
        recv2,
        meet_s,
        meet_r,
        edge_s,
        edge_r,
        edge_image,
        edge_right,
        mrow,
        mom_s,
        mom_r,
        in_sem,
        s1,
        r1,
        s2,
        r2,
        hs,
        hr,
        ms,
        mr_sem,
        known,
    ):
        me = lax.axis_index("fourier")
        z = lax.axis_index("elem")
        up, down = lax.rem(z + 1, NZ), lax.rem(z + NZ - 1, NZ)

        barrier = pltpu.get_barrier_semaphore()

        def far_first(k, size):
            step = (k + 1) // 2
            return size // 2 + step * (1 - 2 * lax.rem(k, 2))

        def peer_f(k):
            row, col, core = me // 8, lax.rem(me // 2, 4), lax.rem(me, 2)
            row = lax.rem(row + far_first(k // 8, 8), 8)
            col = lax.rem(col + far_first(lax.rem(k // 2, 4), 4), 4)
            core = lax.rem(core + 1 + lax.rem(k, 2), 2)
            return row * 8 + col * 2 + core

        def peer_z(k):
            return lax.rem(z + far_first(k, NZ), NZ)

        def greet_f(k, carry):
            pl.semaphore_signal(barrier, inc=1, device_id=(peer_f(k), z), device_id_type=MESH)
            return carry

        for target in (up, down):
            pl.semaphore_signal(barrier, inc=1, device_id=(me, target), device_id_type=MESH)
        lax.fori_loop(0, NF - 1, greet_f, 0, unroll=True)

        loads = [
            pltpu.make_async_copy(src, dst, in_sem.at[i])
            for i, (src, dst) in enumerate(
                [(ma_hbm, ma_s), (mr_hbm, mr_s)]
                + [(ref.at[p, :, pl.ds(128 * h, 128)], to.at[p, h]) for p in range(4) for ref, to in ((ax_hbm, ax), (va_hbm, va), (vr_hbm, vr)) for h in range(2)]
                + [(w256_hbm.at[pl.ds(0, KR_H)], w256.at[pl.ds(0, KR_H)]), (w128_hbm, w128)]
            )
        ]
        late = pltpu.make_async_copy(
            w256_hbm.at[pl.ds(KR_H, 8 - KR_H)], w256.at[pl.ds(KR_H, 8 - KR_H)], in_sem.at[28]
        )
        for load in loads:
            load.start()
        recv2[pl.ds(UNITS * 8, (PADDED - UNITS) * 8), :] = jnp.zeros(
            ((PADDED - UNITS) * 8, 128), F32
        )

        for load in loads[:2]:
            load.wait()
        up_cols = (sublanes((32, COLS)) == lanes((32, COLS)) // 8).astype(F32)
        wide = jnp.dot(
            jnp.concatenate([ma_s[...], mr_s[...]], axis=0),
            up_cols,
            precision=HIGH,
            preferred_element_type=F32,
        )
        metric_a, metric_r = wide[:EZ], wide[EZ:]

        def end_weights(shape):
            place = lanes(shape) % 8
            place = jnp.minimum(place, 7 - place)
            value = jnp.full(shape, float(weights[3]), F32)
            for at in range(3):
                value = jnp.where(place == at, float(weights[at]), value)
            return value

        weight_r = end_weights((1, COLS))
        metric[0] = metric_a
        metric[1] = metric_r
        metric[2] = weight_r / (metric_a * metric_r)
        metric[3] = metric_a / metric_r * weight_r
        metric[4] = metric_r / metric_a
        meet_s[...] = jnp.zeros((8, COLS), F32)
        for row, values in enumerate((metric_a, metric_r)):
            meet_s[2 * row : 2 * row + 1, :] = values[0:1]
            meet_s[2 * row + 1 : 2 * row + 2, :] = values[EZ - 1 :]

        for load in loads[26:]:
            load.wait()

        lane128 = lanes((16, 128))

        row16 = sublanes((EZ, COLS))
        for p in range(4):
            for load in loads[2 + 6 * p : 8 + 6 * p]:
                load.wait()

            def slab_of(ref, j, p=p):
                return jnp.concatenate(
                    [ref[p, h, pl.ds(j, EZ, stride=8), :] for h in range(2)], axis=1
                )

            slabs = [slab_of(ax, j) for j in range(NODES)]
            for j in range(NODES):
                x_s[j * EZ : (j + 1) * EZ, :] = slabs[j]
            x_all = x_s[0:ROWS, :]
            grad_r = right3(x_all, w256[DR_H], w256[DR_L])
            loaded = []
            for j in range(NODES):
                grad_a = along(derivative, slabs, j)
                nonlinear = slab_of(va, j) * (grad_a * metric[0]) + slab_of(vr, j) * (
                    grad_r[j * EZ : (j + 1) * EZ] * metric[1]
                )
                loaded.append(
                    (2.0 * slabs[j] - nonlinear) * ((2.0 * float(weights[j])) * metric[2])
                )
            folded = right2(jnp.concatenate(loaded, axis=0), w256[SR])
            last = folded[ROWS - 1 :]
            for h in range(2):
                send1[X_UNIT * 8 + 2 * p + h : X_UNIT * 8 + 2 * p + h + 1, :] = last[
                    :, 128 * h : 128 * h + 128
                ]
            start = folded[:EZ, :128] + jnp.where(
                row16[:, :128] > 0, roll(folded[7 * EZ :, :128], 1, 0), 0.0
            )
            for j in range(7):
                slab = start if j == 0 else folded[j * EZ : (j + 1) * EZ, :128]
                for h in range(2):
                    send1[pl.ds(64 * j + 2 * p + h, 8, stride=8), :] = slab[8 * h : 8 * h + 8]
            high, low = split(folded[:, 128:])
            packed = dot(w128[RA_B], high) + dot(w128[RA_B], low)
            for h in range(2):
                quarters = [packed[(4 * h + q) * 16 : (4 * h + q + 1) * 16] for q in range(4)]
                for t in range(3):
                    tile = roll(quarters[0], -32 * t, 1)
                    for q in range(1, 4):
                        tile = jnp.where(lane128 >= 32 * q, roll(quarters[q], 32 * (q - t), 1), tile)
                    send1[pl.ds((B_BASE + t) * 8 + 2 * p + h, 16, stride=24), :] = tile
        late.start()

        pl.semaphore_wait(barrier, NF - 1 + 2)

        def exchange(src, dst, at):
            copies = [
                pltpu.make_async_remote_copy(
                    src_ref=src,
                    dst_ref=dst.at[side],
                    send_sem=hs.at[at + side],
                    recv_sem=hr.at[at + side],
                    device_id=(me, target),
                    device_id_type=MESH,
                )
                for side, target in ((0, up), (1, down))
            ]
            for copy in copies:
                copy.start()
            return copies

        def spread_entry(at, reach):
            for step in (reach, NZ - reach):
                pl.semaphore_signal(
                    known.at[at],
                    inc=1,
                    device_id=(me, lax.rem(z + step, NZ)),
                    device_id_type=MESH,
                )
            pl.semaphore_wait(known.at[at], 2)

        def tile_at(index):
            return pl.ds(pl.multiple_of(index * 8, 8), 8)

        def send_plane(unit, slot, target):
            pltpu.make_async_remote_copy(
                src_ref=send1.at[tile_at(unit), :],
                dst_ref=recv1.at[slot, tile_at(me), :],
                send_sem=s1.at[slot],
                recv_sem=r1.at[slot],
                device_id=(target, z),
                device_id_type=MESH,
            ).start()

        def chip_at(k):
            row = lax.rem(me // 8 + far_first(k // 4, 8), 8)
            col = lax.rem(me // 2 + far_first(lax.rem(k, 4), 4), 4)
            return row * 4 + col

        def first_chunk(core):
            def step(k, carry):
                target = 2 * chip_at(k) + core
                send_plane(target, 0, target)
                return carry

            lax.fori_loop(0, NF // 2 - 1, step, 0, unroll=True)
            target = me - lax.rem(me, 2) + core

            @pl.when(target != me)
            def _():
                send_plane(target, 0, target)

        def second_chunk(k, carry):
            chip = chip_at(k)

            @pl.when(2 * chip != me)
            def _():
                send_plane(FIRST + chip, 1, 2 * chip)

            return carry

        first_chunk(0)
        for at, target in enumerate(EXTRA):

            @pl.when(me != target)
            def _(at=at, target=target):
                send_plane(FIRST + NF // 2 + at, 1, target)

        first_chunk(1)
        meets = exchange(meet_s, meet_r, 0)
        lax.fori_loop(0, NF // 2, second_chunk, 0, unroll=True)
        spread_entry(0, 1)
        unit1 = FIRST + me // 2
        owner1 = me % 2 == 0
        for at, target in enumerate(EXTRA):
            unit1 = jnp.where(me == target, FIRST + NF // 2 + at, unit1)
            owner1 = owner1 | (me == target)

        recv1[0, tile_at(me), :] = send1[tile_at(me), :]

        def await_tiles(ref, count, sem):
            view = ref.at[pl.ds(0, count * 8), :]
            pltpu.make_async_copy(view, view, sem).wait()

        def transform(slot, unit):
            x = jnp.concatenate(
                [recv1[slot, pl.ds(h, PLANES, stride=2), :] for h in range(2)], axis=1
            )
            y = left3(w256[C_H], w256[C_L], x)
            for h in range(2):
                send2[slot, pl.ds(h, PLANES, stride=2), :] = y[:, 128 * h : 128 * (h + 1)]

            def send_modes(k, carry):
                target = peer_f(k)
                pltpu.make_async_remote_copy(
                    src_ref=send2.at[slot, tile_at(target), :],
                    dst_ref=recv2.at[tile_at(unit), :],
                    send_sem=s2.at[slot],
                    recv_sem=r2.at[slot],
                    device_id=(target, z),
                    device_id_type=MESH,
                ).start()
                return carry

            lax.fori_loop(0, NF - 1, send_modes, 0, unroll=True)
            recv2[tile_at(unit), :] = send2[slot, tile_at(me), :]

        late.wait()
        await_tiles(recv1.at[0], NF - 1, r1.at[0])
        transform(0, me)
        spread_entry(1, 2)

        @pl.when(owner1)
        def _():
            recv1[1, tile_at(me), :] = send1[tile_at(unit1), :]
            await_tiles(recv1.at[1], NF - 1, r1.at[1])
            transform(1, unit1)

        spread_entry(2, 4)

        await_tiles(recv2, NF - 1, r2.at[0])
        even = sublanes((8, 128)) % 2 == 0
        lane = lanes((8, 128))
        sub = sublanes((8, COLS))
        low_side = sub % 2 == 0
        x_tile = recv2[X_UNIT * 8 : X_UNIT * 8 + 8, :]
        edge_rows = []
        for j in range(8):
            g, q = j // 4, j % 4
            start, end = (8 * j, 8 * j + 7) if j < 7 else (1, X_UNIT)
            part_a = jnp.where(
                even,
                recv2[8 * start : 8 * start + 8, :],
                recv2[8 * end : 8 * end + 8, :] if j < 7 else roll(x_tile, 1, 0),
            )
            pieces = [
                recv2[(B_BASE + 3 * g + t) * 8 : (B_BASE + 3 * g + t) * 8 + 8, :] for t in range(3)
            ]
            part_b = roll(pieces[0], -32 * q, 1)
            for t in range(1, 3):
                part_b = jnp.where(lane >= 32 * t, roll(pieces[t], 32 * (t - q), 1), part_b)
            if j == 7:
                part_b = jnp.where(even, part_b, x_tile)
            edge_rows.append(jnp.concatenate([part_a, part_b], axis=1))
        edge = right2(jnp.concatenate(edge_rows, axis=0), w256[ER])
        along_a = jnp.zeros((8, COLS), F32)
        for j in range(8):
            factor = jnp.where(low_side, float(stiffness[0, j]), float(stiffness[7, j]))
            along_a = along_a + factor * edge[8 * j : 8 * j + 8]
        chosen = jnp.where(low_side, edge[0:8], edge[56:64])
        along_r = right3(chosen, w256[KR_H], w256[KR_L])

        def edge_coef(at):
            return jnp.where(low_side, metric[at, 0:1, :], metric[at, EZ - 1 : EZ, :])

        def shift_of(mode):
            wave = jnp.where(mode == 1, PLANES // 2, mode // 2)
            return 4.0 + (wave.astype(F32) * 0.03125) * (wave.astype(F32) * 0.03125)

        edge_shift = shift_of(4 * me + sub // 2)
        end = float(weights[0])
        image = (
            edge_coef(3) * along_a
            + (end * edge_coef(4)) * along_r
            + edge_shift * (end * edge_coef(2)) * chosen
        )
        edge_s[0:8, :] = join_cols(image)
        edge_s[8:16, :] = chosen
        edges = exchange(edge_s, edge_r, 2)

        for copy in meets:
            copy.wait()
        next_a = jnp.where(low_side, meet_r[0, 1:2, :], meet_r[1, 0:1, :])
        next_r = jnp.where(low_side, meet_r[0, 3:4, :], meet_r[1, 2:3, :])
        corner = jnp.where(low_side, float(stiffness[7, 7]), float(stiffness[0, 0]))
        across = join_cols(
            next_a / next_r * weight_r * (corner * chosen)
            + (end * (next_r / next_a)) * along_r
            + edge_shift * (end * (weight_r / (next_a * next_r))) * chosen
        )

        for copy in edges:
            copy.wait()
        below, above = edge_r[0], edge_r[1]
        edge_image[...] = across + jnp.where(
            low_side, roll(below[0:8], -1, 0), roll(above[0:8], 1, 0)
        )
        edge_right[...] = jnp.where(low_side, roll(below[8:16], -1, 0), roll(above[8:16], 1, 0))

        @pl.when(owner1)
        def _():
            await_tiles(recv2, UNITS - FIRST - 1, r2.at[1])

        @pl.when(jnp.logical_not(owner1))
        def _():
            await_tiles(recv2, UNITS - FIRST, r2.at[1])

        for p in range(4):
            for h in range(2):
                pieces = [
                    recv2[pl.ds((B_BASE + t) * 8 + 2 * p + h, 16, stride=24), :] for t in range(3)
                ]
                for q in range(4):
                    part_b = roll(pieces[0], -32 * q, 1)
                    for t in range(1, 3):
                        part_b = jnp.where(
                            lane128 >= 32 * t, roll(pieces[t], 32 * (t - q), 1), part_b
                        )
                    if h == 0 and q == 0:
                        part_b = jnp.where(
                            sublanes((16, 128)) == 14, x_tile[2 * p + 1 : 2 * p + 2, :], part_b
                        )
                    packed_b[p, (4 * h + q) * 16 : (4 * h + q + 1) * 16, :] = part_b

        lane_r = lanes((1, COLS))
        inner_r = jnp.where(
            ((lane_r % 8 == 7) & (lane_r < COLS - 1)) | ((lane_r % 8 == 0) & (lane_r > 0)), 0.5, 1.0
        )

        def slabs_of(field):
            return [field[j * EZ : (j + 1) * EZ] for j in range(NODES)]

        def operate(slabs, along_r, shift):
            heavy = shift * metric[2]
            return [
                metric[3] * along(stiffness, slabs, j)
                + float(weights[j]) * (metric[4] * along_r[j] + heavy * slabs[j])
                for j in range(NODES)
            ]

        def product(left, right, ends):
            total = ends * (left[0] * right[0] + left[7] * right[7])
            for j in range(1, 7):
                total = total + left[j] * right[j]
            return total

        def total(field):
            row = jnp.sum(field, axis=0, keepdims=True)
            return row[:, :128] + row[:, 128:]

        for p in range(4):
            left_cols = []
            for j in range(7):
                left_cols += [recv2[pl.ds(64 * j + 2 * p + h, 8, stride=8), :] for h in range(2)]
            first_slab = jnp.concatenate(left_cols[:2], axis=0)
            left_cols.append(
                jnp.where(
                    row16[:, :128] == EZ - 1, x_tile[2 * p : 2 * p + 1, :], roll(first_slab, -1, 0)
                )
            )
            high, low = split(packed_b[p])
            right_cols = dot(w128[EA_B], high) + dot(w128[EA_B], low)
            x_s[ROWS * p : ROWS * (p + 1), :] = jnp.concatenate(
                [jnp.concatenate(left_cols, axis=0), right_cols], axis=1
            )
        x_s[...] = right2(x_s[...], w256[ER])
        for p in range(4):
            top = ROWS * p
            x_s[top : top + 8, :] = x_s[top : top + 8, :] + jnp.where(
                sub == 0, edge_right[2 * p : 2 * p + 1, :], 0.0
            )
            top = ROWS * (p + 1) - 8
            x_s[top : top + 8, :] = x_s[top : top + 8, :] + jnp.where(
                sub == 7, edge_right[2 * p + 1 : 2 * p + 2, :], 0.0
            )
        r_s[...] = right3(x_s[...], w256[KR_H], w256[KR_L])
        for p in range(4):
            at = ROWS * p
            b_s[p] = x_s[at : at + ROWS, :]
            right = slabs_of(b_s[p])
            raw = operate(right, slabs_of(r_s[at : at + ROWS, :]), shift_of(4 * me + p))
            joined = join_cols(jnp.concatenate(raw, axis=0))
            low_slab, high_slab = joined[:EZ], joined[7 * EZ :]
            bottom = low_slab + jnp.where(
                row16 == 0, edge_image[2 * p : 2 * p + 1, :], roll(high_slab, 1, 0)
            )
            top = high_slab + jnp.where(
                row16 == EZ - 1, edge_image[2 * p + 1 : 2 * p + 2, :], roll(low_slab, -1, 0)
            )
            joined = jnp.concatenate([bottom, joined[EZ : 7 * EZ], top], axis=0)
            v_s[p] = joined
            joined = slabs_of(joined)
            mrow[p, 0:1, :] = total(product(right, right, 0.5) * inner_r)
            mrow[p, 1:2, :] = total(product(right, raw, 1.0))
            mrow[p, 2:3, :] = total(product(joined, joined, 0.5) * inner_r)
            mrow[p, 4:8, :] = jnp.zeros((4, 128), F32)
        for p in range(4):
            x_s[ROWS * p : ROWS * (p + 1), :] = v_s[p]
        r_s[...] = right3(x_s[...], w256[KR_H], w256[KR_L])
        for p in range(4):
            at = ROWS * p
            joined = slabs_of(v_s[p])
            raw = operate(joined, slabs_of(r_s[at : at + ROWS, :]), shift_of(4 * me + p))
            mrow[p, 3:4, :] = total(product(joined, raw, 1.0))

        sums = jnp.sum(
            jnp.concatenate([mrow[p] for p in range(4)], axis=0), axis=1, keepdims=True
        )
        row32, lane32 = sublanes((32, 128)), lanes((32, 128))
        mine = (row32 % 8 < 4) & (lane32 // 8 == (row32 // 8) * 4 + row32 % 8)
        moments = jnp.sum(jnp.where(mine, sums, 0.0), axis=0, keepdims=True)
        mom_s[...] = moments
        mom_r[z] = moments

        def send_moments(k, carry):
            pltpu.make_async_remote_copy(
                src_ref=mom_s,
                dst_ref=mom_r.at[z],
                send_sem=ms,
                recv_sem=mr_sem,
                device_id=(me, peer_z(k)),
                device_id_type=MESH,
            ).start()
            return carry

        lax.fori_loop(0, NZ - 1, send_moments, 0, unroll=True)
        view = mom_r.at[pl.ds(0, NZ - 1)]
        pltpu.make_async_copy(view, view, mr_sem).wait()
        pooled = mom_r[0]
        for at in range(1, NZ):
            pooled = pooled + mom_r[at]
        m0 = pooled
        m1, m2, m3 = (roll(pooled, -8 * k, 1) for k in range(1, 4))
        alpha0 = m0 / m1
        norm1 = alpha0 * alpha0 * m2 - m0
        gain = 1.0 + norm1 / m0
        curve = gain * gain * m1 - 2.0 * gain * alpha0 * m2 + alpha0 * alpha0 * m3
        alpha1 = norm1 / curve
        on_right = alpha0 + alpha1 * gain
        on_image = -alpha1 * alpha0
        lane1 = lanes((1, 128))
        for p in range(4):
            pick = lane1 == 32 * p
            first = jnp.sum(jnp.where(pick, on_right, 0.0), axis=1, keepdims=True)
            second = jnp.sum(jnp.where(pick, on_image, 0.0), axis=1, keepdims=True)
            factors[p] = jnp.concatenate(
                [first + jnp.zeros((1, 128), F32), second + jnp.zeros((1, 128), F32)]
                + [jnp.zeros((6, 128), F32)],
                axis=0,
            )

        pltpu.make_async_copy(view, view, ms).wait()
        await_tiles(recv1.at[0], NF - 1, s1.at[0])
        await_tiles(recv2, NF - 1, s2.at[0])

        @pl.when(owner1)
        def _():
            await_tiles(recv1.at[1], UNITS - FIRST - 1, s1.at[1])
            await_tiles(recv2, NF - 1, s2.at[1])

        @pl.when(jnp.logical_not(owner1))
        def _():
            await_tiles(recv1.at[1], UNITS - FIRST, s1.at[1])

    return kernel


def combine(right, image, factors, out, slots, sems):
    copies = []
    for p in range(4):
        mixed = factors[p, 0:1, 0:1] * right[p] + factors[p, 1:2, 0:1] * image[p]
        for h in range(2):
            for j in range(NODES):
                slots[p, h, pl.ds(j, EZ, stride=8), :] = mixed[
                    j * EZ : (j + 1) * EZ, 128 * h : 128 * h + 128
                ]
            copy = pltpu.make_async_copy(
                slots.at[p, h], out.at[p, :, pl.ds(128 * h, 128)], sems.at[2 * p + h]
            )
            copy.start()
            copies.append(copy)
    for copy in copies:
        copy.wait()


def solution(mesh):
    w256, w128, weights, derivative, stiffness = tables()
    kernel = make_kernel(weights, derivative, stiffness)

    def shards(vel_az, vel_rad, axial, metric_az, metric_rad):
        field = (4, ROWS, COLS)
        solved = pl.pallas_call(
            kernel,
            out_shape=(pltpu.VMEM(field, F32), pltpu.VMEM(field, F32), pltpu.VMEM((4, 8, 128), F32)),
            in_specs=[pl.BlockSpec(memory_space=pltpu.HBM)] * 7,
            out_specs=[pl.BlockSpec(memory_space=pltpu.VMEM)] * 3,
            scratch_shapes=[
                pltpu.VMEM((4, 2, ROWS, 128), F32),
                pltpu.VMEM((4, 2, ROWS, 128), F32),
                pltpu.VMEM((4, 2, ROWS, 128), F32),
                pltpu.VMEM((EZ, 32), F32),
                pltpu.VMEM((EZ, 32), F32),
                pltpu.VMEM(w256.shape, BF16),
                pltpu.VMEM(w128.shape, BF16),
                pltpu.VMEM((5, EZ, COLS), F32),
                pltpu.VMEM((4 * ROWS, COLS), F32),
                pltpu.VMEM((4 * ROWS, COLS), F32),
                pltpu.VMEM((4, ROWS, 128), F32),
                pltpu.VMEM((PADDED * 8, 128), F32),
                pltpu.VMEM((2, NF * 8, 128), F32),
                pltpu.VMEM((2, NF * 8, 128), F32),
                pltpu.VMEM((PADDED * 8, 128), F32),
                pltpu.VMEM((8, COLS), F32),
                pltpu.VMEM((2, 8, COLS), F32),
                pltpu.VMEM((16, COLS), F32),
                pltpu.VMEM((2, 16, COLS), F32),
                pltpu.VMEM((8, COLS), F32),
                pltpu.VMEM((8, COLS), F32),
                pltpu.VMEM((4, 8, 128), F32),
                pltpu.VMEM((1, 128), F32),
                pltpu.VMEM((NZ, 1, 128), F32),
                pltpu.SemaphoreType.DMA((29,)),
                pltpu.SemaphoreType.DMA((2,)),
                pltpu.SemaphoreType.DMA((2,)),
                pltpu.SemaphoreType.DMA((2,)),
                pltpu.SemaphoreType.DMA((2,)),
                pltpu.SemaphoreType.DMA((4,)),
                pltpu.SemaphoreType.DMA((4,)),
                pltpu.SemaphoreType.DMA(()),
                pltpu.SemaphoreType.DMA(()),
                pltpu.SemaphoreType.REGULAR((3,)),
            ],
            compiler_params=pltpu.CompilerParams(
                collective_id=0, has_side_effects=True, vmem_limit_bytes=63488 * 1024
            ),
        )(
            vel_az,
            vel_rad,
            axial,
            metric_az,
            metric_rad,
            jnp.asarray(w256),
            jnp.asarray(w128),
        )
        return pl.pallas_call(
            combine,
            out_shape=jax.ShapeDtypeStruct(field, F32),
            in_specs=[pl.BlockSpec(memory_space=pltpu.VMEM)] * 3,
            out_specs=pl.BlockSpec(memory_space=pltpu.HBM),
            scratch_shapes=[pltpu.VMEM((4, 2, ROWS, 128), F32), pltpu.SemaphoreType.DMA((8,))],
            compiler_params=pltpu.CompilerParams(vmem_limit_bytes=16 * 2**20),
        )(*solved)

    spec = P("fourier", "elem", None)
    metric_spec = P("elem", None)
    return jax.shard_map(
        shards,
        mesh=mesh,
        in_specs=(spec, spec, spec, metric_spec, metric_spec),
        out_specs=spec,
        check_vma=False,
    )
```
